32 devices in a mesh: dp: 8 (over y, x, core), tensor: 4 (over z).
Axes of the slice: x: 2, y: 2, z: 4, core: 2. Of those that a mesh axis runs over, the one named last changes fastest.
Arguments:
- prefix_tokens: bfloat16 [16, 256, 5120], P('dp'), may hold values from -6 to 6
- prefix_len: int32 [16], P('dp'), may hold values from 64 to 256, as said below
- causal_start: int32 [16], P('dp'), may hold values from 32 to 64
- span_sample: int32 [64], P('dp'), may hold values from 0 to 1
- bb_wq: bfloat16 [5120, 4096], P('dp', 'tensor'), may hold values from -4 to 4
- bb_wk: bfloat16 [5120, 1024], P('dp', 'tensor'), may hold values from -1 to 1
- bb_wv: bfloat16 [5120, 1024], P('dp', 'tensor'), may hold values from -0.078125 to 0.078125
- bb_wo: bfloat16 [4096, 5120], P('tensor', 'dp'), may hold values from -0.09375 to 0.09375
- action_tokens: bfloat16 [64, 50, 1024], P('dp'), may hold values from -6 to 6
- ex_wq: bfloat16 [1024, 2048], P(None, 'tensor'), may hold values from -8 to 8
- ex_wk: bfloat16 [1024, 1024], P(None, 'tensor'), may hold values from -1 to 1
- ex_wv: bfloat16 [1024, 1024], P(None, 'tensor'), may hold values from -0.1875 to 0.1875
- ex_wo: bfloat16 [2048, 1024], P('tensor'), may hold values from -0.125 to 0.125
- action_cot: bfloat16 [64, 50, 1024], P('dp'), may hold values from -6 to 6
Outputs:
- prefix_out: bfloat16 [16, 256, 5120], P('dp', None, 'tensor')
- grad_wq: float32 [1024, 2048], P(None, 'tensor')
- grad_wk: float32 [1024, 1024], P(None, 'tensor')
- grad_wv: float32 [1024, 1024], P(None, 'tensor')
- grad_wo: float32 [2048, 1024], P('tensor')
The draws below stay inside these ranges and needn't reach their ends.
Inputs may be any that keep to these rules, and one draw needn't show every extreme that they name: `prefix_len`: some sample has all 256 positions valid.
All inputs are finite; a program needn't handle non-finite values.
Results may differ from the reference program's by a relative error of at most 0.003.
The reference program's roundings to bfloat16 on the way count: a program that leaves them out, or rounds other values in their place, can miss the bound.
Values may be sent and summed in bfloat16 or wider, within the bound.
No kernel may reach another device: no remote copies, remote signals or barrier semaphores. Data moves between devices by JAX's collectives and lax.ppermute only.
A program may use at most 192 MiB of HBM per device.

```python
import math
import jax
import jax.numpy as jnp
from jax import lax

D = 5120
HD = 128
BHEADS = 32
KVH = 8
EW = 1024
EHEADS = 16
STEPS = 50
PREFIX = 256
SAMP_DEV = 2
SPAN_DEV = 8
SAMPLES = 16
SPANS = 64
QW = 4096
KW = 1024
EQ = 2048


def draw_prefix_len(key, part):
    key = jax.random.fold_in(key, 11)
    lengths = jax.random.randint(key, (SAMPLES,), PREFIX // 4, PREFIX + 1, dtype=jnp.int32)
    return lengths.at[0].set(PREFIX)


def backbone_key_base(key):
    return jnp.clip(jax.random.normal(jax.random.fold_in(key, 101), (D, KW), jnp.float32), -6.0, 6.0)


def expert_key_base(key):
    return jnp.clip(jax.random.normal(jax.random.fold_in(key, 102), (EW, KW), jnp.float32), -6.0, 6.0)


def draw_prefix_tokens(key, part):
    key = jax.random.fold_in(key, 23)
    values = jax.random.normal(key, (SAMPLES, PREFIX, D), jnp.float32)
    return jnp.clip(values, -6.0, 6.0).astype(jnp.bfloat16)


def draw_action_tokens(key, part):
    key = jax.random.fold_in(key, 24)
    values = jax.random.normal(key, (SPANS, STEPS, EW), jnp.float32)
    return jnp.clip(values, -6.0, 6.0).astype(jnp.bfloat16)


def draw_bb_wk(key, part):
    base = backbone_key_base(key)
    weight = base * D ** (-0.5)
    return jnp.clip(weight, -1.0, 1.0).astype(jnp.bfloat16)


def draw_bb_wq(key, part):
    key = jax.random.fold_in(key, 22)
    weight = jnp.clip(jax.random.normal(key, (D, QW), jnp.float32), -6.0, 6.0) * D ** (-0.5)
    return jnp.clip(weight, -4.0, 4.0).astype(jnp.bfloat16)


def draw_ex_wk(key, part):
    base = expert_key_base(key)
    weight = base * EW ** (-0.5)
    return jnp.clip(weight, -1.0, 1.0).astype(jnp.bfloat16)


def draw_ex_wq(key, part):
    key = jax.random.fold_in(key, 32)
    weight = jnp.clip(jax.random.normal(key, (EW, EQ), jnp.float32), -6.0, 6.0) * EW ** (-0.5)
    return jnp.clip(weight, -8.0, 8.0).astype(jnp.bfloat16)


def set_ends(result, stream_key, least, high):
    longest = result.shape.index(max(result.shape))
    spots = []
    for shift in (0, 1):
        where = [jax.random.randint(jax.random.fold_in(stream_key, axis), (), 0, length) for axis, length in enumerate(result.shape)]
        where[longest] = (where[longest] + shift) % result.shape[longest]
        spots.append(tuple(where))
    return result.at[spots[0]].set(least).at[spots[1]].set(high)


def block_levels(rng, extent, cuts, least, top_value):
    def one(axis_at, blocks):
        steps = jax.random.uniform(jax.random.fold_in(jax.random.fold_in(rng, 6), axis_at), (blocks,), jnp.float32, least / len(cuts), top_value / len(cuts))
        return jnp.repeat(jnp.exp(steps), extent[axis_at] // blocks).reshape((-1,) + (1,) * (len(extent) - axis_at - 1))

    gain = one(*cuts[0])
    for cut in cuts[1:]:
        gain = gain * one(*cut)
    return gain


def gaussian(own_key, dims, spread, limit, split=(), kind=jnp.bfloat16):
    array = spread * jax.random.normal(own_key, dims, jnp.float32)
    if split:
        array = array * block_levels(own_key, dims, split, -0.22, 0.18)
    return jnp.clip(array, -limit, limit).astype(kind)


def setup_inputs(seed: int = 0) -> dict:
    key_list = jax.random.split(jax.random.key(seed), 15)
    prefix_tokens = draw_prefix_tokens(jax.random.fold_in(key_list[14], 71), 0)
    prefix_len = draw_prefix_len(jax.random.fold_in(key_list[14], 71), 0)
    causal_start = set_ends(jax.random.randint(key_list[2], (SAMPLES,), PREFIX // 8, PREFIX // 4 + 1), jax.random.fold_in(key_list[2], 1), PREFIX // 8, (PREFIX // 4 + 1) - 1).astype(jnp.int32)
    span_sample = set_ends(jax.random.randint(key_list[3], (SPANS,), 0, SAMP_DEV), jax.random.fold_in(key_list[3], 1), 0, SAMP_DEV - 1).astype(jnp.int32)
    bb_wq = draw_bb_wq(jax.random.fold_in(key_list[14], 71), 0)
    bb_wk = draw_bb_wk(jax.random.fold_in(key_list[14], 71), 0)
    bb_wv = gaussian(key_list[6], (D, KW), D ** -0.5, 0.078125, ((0, 8), (1, 4)))
    bb_wo = gaussian(key_list[7], (QW, D), QW ** -0.5, 0.09375, ((0, 4), (1, 8)))
    action_tokens = draw_action_tokens(jax.random.fold_in(key_list[14], 71), 0)
    ex_wq = draw_ex_wq(jax.random.fold_in(key_list[14], 71), 0)
    ex_wk = draw_ex_wk(jax.random.fold_in(key_list[14], 71), 0)
    ex_wv = gaussian(key_list[11], (EW, KW), EW ** -0.5, 0.1875, ((1, 4),))
    ex_wo = gaussian(key_list[12], (EQ, EW), EQ ** -0.5, 0.125, ((0, 4),))
    action_cot = gaussian(key_list[13], (SPANS, STEPS, EW), 1.0, 6.0, ((0, 8),))
    return {"prefix_tokens": prefix_tokens, "prefix_len": prefix_len, "causal_start": causal_start, "span_sample": span_sample, "bb_wq": bb_wq, "bb_wk": bb_wk, "bb_wv": bb_wv, "bb_wo": bb_wo, "action_tokens": action_tokens, "ex_wq": ex_wq, "ex_wk": ex_wk, "ex_wv": ex_wv, "ex_wo": ex_wo, "action_cot": action_cot}


def normalize(tokens):
    values = tokens.astype(jnp.float32)
    scale = lax.rsqrt(lax.optimization_barrier(jnp.mean(values * values, axis=-1, keepdims=True)) + 1e-06)
    return values * scale

def reference(prefix_tokens, prefix_len, causal_start, span_sample, bb_wq, bb_wk, bb_wv, bb_wo, action_tokens, ex_wq, ex_wk, ex_wv, ex_wo, action_cot):
    factor = 1.0 / math.sqrt(HD)
    group = BHEADS // KVH
    egroup = EHEADS // KVH

    def backbone(item):
        tokens, length, cstart = item
        normed = normalize(tokens).astype(jnp.bfloat16)
        query = jnp.dot(normed, bb_wq, preferred_element_type=jnp.float32).astype(jnp.bfloat16).reshape(PREFIX, KVH, group, HD)
        keys = jnp.dot(normed, bb_wk, preferred_element_type=jnp.float32).astype(jnp.bfloat16).reshape(PREFIX, KVH, HD)
        values = jnp.dot(normed, bb_wv, preferred_element_type=jnp.float32).astype(jnp.bfloat16).reshape(PREFIX, KVH, HD)
        scores = jnp.einsum('igeh,jgh->geij', query.astype(jnp.float32), keys.astype(jnp.float32)) * factor
        places = jnp.arange(PREFIX, dtype=jnp.int32)
        visible = (places[None, :] < length) & ((places[None, :] < cstart) | (places[None, :] <= places[:, None]))
        scores = jnp.where(visible, scores, -1e+30)
        top = lax.optimization_barrier(jnp.max(scores, axis=-1, keepdims=True))
        weights = jnp.where(visible, jnp.exp(scores - top), 0.0)
        weights = (weights / lax.optimization_barrier(jnp.sum(weights, axis=-1, keepdims=True))).astype(jnp.bfloat16)
        context = jnp.einsum('geij,jgh->igeh', weights.astype(jnp.float32), values.astype(jnp.float32)).astype(jnp.bfloat16).reshape(PREFIX, QW)
        attended = jnp.dot(context, bb_wo, preferred_element_type=jnp.float32)
        return ((tokens.astype(jnp.float32) + attended).astype(jnp.bfloat16), keys, values)
    prefix_out, all_keys, all_values = lax.map(backbone, (prefix_tokens, prefix_len, causal_start))
    sample_of = jnp.arange(SPANS, dtype=jnp.int32) // SPAN_DEV * SAMP_DEV + span_sample

    def expert(item):
        action, cotangent, sample = item
        pre_keys = lax.dynamic_index_in_dim(all_keys, sample, 0, keepdims=False).astype(jnp.float32)
        pre_values = lax.dynamic_index_in_dim(all_values, sample, 0, keepdims=False).astype(jnp.float32)
        length = lax.dynamic_index_in_dim(prefix_len, sample, 0, keepdims=False)
        query = jnp.dot(action, ex_wq, preferred_element_type=jnp.float32).astype(jnp.bfloat16).reshape(STEPS, KVH, egroup, HD).astype(jnp.float32)
        own_keys = jnp.dot(action, ex_wk, preferred_element_type=jnp.float32).astype(jnp.bfloat16).reshape(STEPS, KVH, HD).astype(jnp.float32)
        own_values = jnp.dot(action, ex_wv, preferred_element_type=jnp.float32).astype(jnp.bfloat16).reshape(STEPS, KVH, HD).astype(jnp.float32)
        valid = jnp.arange(PREFIX, dtype=jnp.int32) < length
        score_pre = jnp.einsum('tgeh,pgh->getp', query, pre_keys) * factor
        score_pre = jnp.where(valid, score_pre, -1e+30)
        score_own = jnp.einsum('tgeh,ugh->getu', query, own_keys) * factor
        top = jnp.maximum(lax.optimization_barrier(jnp.max(score_pre, axis=-1)), lax.optimization_barrier(jnp.max(score_own, axis=-1)))[..., None]
        exp_pre = jnp.where(valid, jnp.exp(score_pre - top), 0.0)
        exp_own = jnp.exp(score_own - top)
        total = lax.optimization_barrier(jnp.sum(exp_pre, axis=-1, keepdims=True)) + lax.optimization_barrier(jnp.sum(exp_own, axis=-1, keepdims=True))
        prob_pre = exp_pre / total
        prob_own = exp_own / total
        half_pre = prob_pre.astype(jnp.bfloat16).astype(jnp.float32)
        half_own = prob_own.astype(jnp.bfloat16).astype(jnp.float32)
        context = (jnp.einsum('getp,pgh->tgeh', half_pre, pre_values) + jnp.einsum('getu,ugh->tgeh', half_own, own_values)).astype(jnp.bfloat16)
        dcontext = jnp.dot(cotangent, ex_wo.T, preferred_element_type=jnp.float32).astype(jnp.bfloat16).reshape(STEPS, KVH, egroup, HD).astype(jnp.float32)
        dprob_pre = jnp.einsum('tgeh,pgh->getp', dcontext, pre_values)
        dprob_own = jnp.einsum('tgeh,ugh->getu', dcontext, own_values)
        delta = (lax.optimization_barrier(jnp.sum(prob_pre * dprob_pre, axis=-1)) + lax.optimization_barrier(jnp.sum(prob_own * dprob_own, axis=-1)))[..., None]
        dscore_pre = (prob_pre * (dprob_pre - delta) * factor).astype(jnp.bfloat16).astype(jnp.float32)
        dscore_own = (prob_own * (dprob_own - delta) * factor).astype(jnp.bfloat16).astype(jnp.float32)
        dquery = (jnp.einsum('getp,pgh->tgeh', dscore_pre, pre_keys) + jnp.einsum('getu,ugh->tgeh', dscore_own, own_keys)).astype(jnp.bfloat16)
        dkeys = jnp.einsum('getu,tgeh->ugh', dscore_own, query).astype(jnp.bfloat16)
        dvalues = jnp.einsum('getu,tgeh->ugh', half_own, dcontext).astype(jnp.bfloat16)
        return (context.reshape(STEPS, EQ), dquery.reshape(STEPS, EQ), dkeys.reshape(STEPS, KW), dvalues.reshape(STEPS, KW))
    context, dquery, dkeys, dvalues = lax.map(expert, (action_tokens, action_cot, sample_of))
    action_flat = action_tokens.reshape(SPANS * STEPS, EW)
    cot_flat = action_cot.reshape(SPANS * STEPS, EW)
    grad_wq = jnp.dot(action_flat.T, dquery.reshape(SPANS * STEPS, EQ), preferred_element_type=jnp.float32)
    grad_wk = jnp.dot(action_flat.T, dkeys.reshape(SPANS * STEPS, KW), preferred_element_type=jnp.float32)
    grad_wv = jnp.dot(action_flat.T, dvalues.reshape(SPANS * STEPS, KW), preferred_element_type=jnp.float32)
    grad_wo = jnp.dot(context.reshape(SPANS * STEPS, EQ).T, cot_flat, preferred_element_type=jnp.float32)
    return (prefix_out, grad_wq, grad_wk, grad_wv, grad_wo)
```

```python
import functools
import math

import jax
import jax.numpy as jnp
from jax import lax
from jax.experimental import pallas as pl
from jax.experimental.pallas import tpu as pltpu
from jax.sharding import PartitionSpec as P

HD = 128
STEPS = 50


def general_body(
    prefix_tokens,
    prefix_len,
    causal_start,
    span_sample,
    bb_wq,
    bb_wk,
    bb_wv,
    bb_wo,
    action_tokens,
    ex_wq,
    ex_wk,
    ex_wv,
    ex_wo,
    action_cot,
):
    samples, positions, width = prefix_tokens.shape
    factor = 1.0 / math.sqrt(HD)
    kv_local = bb_wk.shape[1] // HD
    group = bb_wq.shape[1] // bb_wk.shape[1]
    egroup = ex_wq.shape[1] // ex_wk.shape[1]
    count = samples * positions
    flat = prefix_tokens.reshape(count, width)
    widened = flat.astype(jnp.float32)
    normed = (
        widened * lax.rsqrt(jnp.mean(widened * widened, axis=-1, keepdims=True) + 1e-06)
    ).astype(jnp.bfloat16)
    pieces = (
        lax.all_gather(bb_wq, "dp", axis=0, tiled=True),
        lax.all_gather(bb_wk, "dp", axis=0, tiled=True),
        lax.all_gather(bb_wv, "dp", axis=0, tiled=True),
    )
    query_sum, key_sum, value_sum = tuple(
        (jnp.dot(normed, piece, preferred_element_type=jnp.float32) for piece in pieces)
    )
    query = query_sum.astype(jnp.bfloat16).reshape(samples, positions, kv_local, group, HD)
    keys = key_sum.astype(jnp.bfloat16).reshape(samples, positions, kv_local, HD)
    values = value_sum.astype(jnp.bfloat16).reshape(samples, positions, kv_local, HD)
    scores = (
        jnp.einsum("sigeh,sjgh->sgeij", query, keys, preferred_element_type=jnp.float32) * factor
    )
    places = jnp.arange(positions, dtype=jnp.int32)
    length_view = prefix_len[:, None, None, None, None]
    start_view = causal_start[:, None, None, None, None]
    visible = (places[None, None, None, None, :] < length_view) & (
        (places[None, None, None, None, :] < start_view)
        | (places[None, None, None, None, :] <= places[None, None, None, :, None])
    )
    scores = jnp.where(visible, scores, -1e30)
    top = jnp.max(scores, axis=-1, keepdims=True)
    weights = jnp.where(visible, jnp.exp(scores - top), 0.0)
    weights = (weights / jnp.sum(weights, axis=-1, keepdims=True)).astype(jnp.bfloat16)
    context = (
        jnp.einsum("sgeij,sjgh->sigeh", weights, values, preferred_element_type=jnp.float32)
        .astype(jnp.bfloat16)
        .reshape(count, bb_wq.shape[1])
    )
    partial_out = jnp.dot(
        context, lax.all_gather(bb_wo, "dp", axis=1, tiled=True), preferred_element_type=jnp.float32
    )
    summed = lax.psum_scatter(partial_out, "tensor", scatter_dimension=1, tiled=True)
    share = summed.shape[1]
    residual = lax.dynamic_slice_in_dim(widened, lax.axis_index("tensor") * share, share, 1)
    prefix_out = (residual + summed).astype(jnp.bfloat16).reshape(samples, positions, share)
    spans = action_tokens.shape[0]
    rows = spans * STEPS
    action_flat = action_tokens.reshape(rows, action_tokens.shape[2])
    cot_flat = action_cot.reshape(rows, action_cot.shape[2])
    pre_keys = jnp.take(keys, span_sample, axis=0)
    pre_values = jnp.take(values, span_sample, axis=0)
    span_length = jnp.take(prefix_len, span_sample, axis=0)
    equery = (
        jnp.dot(action_flat, ex_wq, preferred_element_type=jnp.float32)
        .astype(jnp.bfloat16)
        .reshape(spans, STEPS, kv_local, egroup, HD)
    )
    own_keys = (
        jnp.dot(action_flat, ex_wk, preferred_element_type=jnp.float32)
        .astype(jnp.bfloat16)
        .reshape(spans, STEPS, kv_local, HD)
    )
    own_values = (
        jnp.dot(action_flat, ex_wv, preferred_element_type=jnp.float32)
        .astype(jnp.bfloat16)
        .reshape(spans, STEPS, kv_local, HD)
    )
    valid = (places[None, :] < span_length[:, None])[:, None, None, None, :]
    score_pre = (
        jnp.einsum("ctgeh,cpgh->cgetp", equery, pre_keys, preferred_element_type=jnp.float32)
        * factor
    )
    score_pre = jnp.where(valid, score_pre, -1e30)
    score_own = (
        jnp.einsum("ctgeh,cugh->cgetu", equery, own_keys, preferred_element_type=jnp.float32)
        * factor
    )
    peak = jnp.maximum(jnp.max(score_pre, axis=-1), jnp.max(score_own, axis=-1))[..., None]
    exp_pre = jnp.where(valid, jnp.exp(score_pre - peak), 0.0)
    exp_own = jnp.exp(score_own - peak)
    total = jnp.sum(exp_pre, axis=-1, keepdims=True) + jnp.sum(exp_own, axis=-1, keepdims=True)
    prob_pre = exp_pre / total
    prob_own = exp_own / total
    half_pre = prob_pre.astype(jnp.bfloat16)
    half_own = prob_own.astype(jnp.bfloat16)
    econtext = (
        jnp.einsum("cgetp,cpgh->ctgeh", half_pre, pre_values, preferred_element_type=jnp.float32)
        + jnp.einsum("cgetu,cugh->ctgeh", half_own, own_values, preferred_element_type=jnp.float32)
    ).astype(jnp.bfloat16)
    econtext_flat = econtext.reshape(rows, ex_wq.shape[1])
    grad_out_local = jnp.einsum(
        "ti,tj->ij", econtext_flat, cot_flat, preferred_element_type=jnp.float32
    )
    dcontext = (
        jnp.einsum("tj,ij->ti", cot_flat, ex_wo, preferred_element_type=jnp.float32)
        .astype(jnp.bfloat16)
        .reshape(spans, STEPS, kv_local, egroup, HD)
    )
    dprob_pre = jnp.einsum(
        "ctgeh,cpgh->cgetp", dcontext, pre_values, preferred_element_type=jnp.float32
    )
    dprob_own = jnp.einsum(
        "ctgeh,cugh->cgetu", dcontext, own_values, preferred_element_type=jnp.float32
    )
    delta = (jnp.sum(prob_pre * dprob_pre, axis=-1) + jnp.sum(prob_own * dprob_own, axis=-1))[
        ..., None
    ]
    dscore_pre = (prob_pre * (dprob_pre - delta) * factor).astype(jnp.bfloat16)
    dscore_own = (prob_own * (dprob_own - delta) * factor).astype(jnp.bfloat16)
    dquery = (
        jnp.einsum("cgetp,cpgh->ctgeh", dscore_pre, pre_keys, preferred_element_type=jnp.float32)
        + jnp.einsum("cgetu,cugh->ctgeh", dscore_own, own_keys, preferred_element_type=jnp.float32)
    ).astype(jnp.bfloat16)
    dkeys = jnp.einsum(
        "cgetu,ctgeh->cugh", dscore_own, equery, preferred_element_type=jnp.float32
    ).astype(jnp.bfloat16)
    dvalues = jnp.einsum(
        "cgetu,ctgeh->cugh", half_own, dcontext, preferred_element_type=jnp.float32
    ).astype(jnp.bfloat16)
    grad_query_local = jnp.einsum(
        "ti,tj->ij",
        action_flat,
        dquery.reshape(rows, ex_wq.shape[1]),
        preferred_element_type=jnp.float32,
    )
    grad_key_local = jnp.einsum(
        "ti,tj->ij",
        action_flat,
        dkeys.reshape(rows, ex_wk.shape[1]),
        preferred_element_type=jnp.float32,
    )
    grad_value_local = jnp.einsum(
        "ti,tj->ij",
        action_flat,
        dvalues.reshape(rows, ex_wv.shape[1]),
        preferred_element_type=jnp.float32,
    )
    grad_wq, grad_wk, grad_wv, grad_wo = lax.psum(
        (grad_query_local, grad_key_local, grad_value_local, grad_out_local), "dp"
    )
    return (prefix_out, grad_wq, grad_wk, grad_wv, grad_wo)


NEG = -1e30
PAD = 64
HIGH = 56 * 1024 * 1024


def params():
    return pltpu.CompilerParams(vmem_limit_bytes=HIGH)


def cost(flops, moved):
    return pl.CostEstimate(flops=int(flops), bytes_accessed=int(moved), transcendentals=0)


def whole():
    return pl.BlockSpec(memory_space=pltpu.VMEM)


def nt(a, b):
    return lax.dot_general(a, b, (((1,), (1,)), ((), ())), preferred_element_type=jnp.float32)


def tn(a, b):
    return lax.dot_general(a, b, (((0,), (0,)), ((), ())), preferred_element_type=jnp.float32)


def nn(a, b):
    return jnp.dot(a, b, preferred_element_type=jnp.float32)


def norm_kernel(meta, x_ref, out_ref):
    chip = meta[0]
    parts, rows, wide = out_ref.shape
    x = x_ref[...].astype(jnp.float32)
    scale = lax.rsqrt(jnp.mean(x * x, axis=-1, keepdims=True) + 1e-06)
    for j in range(parts):
        at = pl.multiple_of((chip ^ j) * wide, wide)
        piece = x_ref[:, pl.ds(at, wide)].astype(jnp.float32)
        out_ref[j] = (piece * scale).astype(jnp.bfloat16)


def normalise(meta, flat, parts):
    count, width = flat.shape
    block = 128
    return pl.pallas_call(
        norm_kernel,
        grid_spec=pltpu.PrefetchScalarGridSpec(
            num_scalar_prefetch=1,
            grid=(count // block,),
            in_specs=[pl.BlockSpec((block, width), lambda i, m: (i, 0))],
            out_specs=pl.BlockSpec((parts, block, width // parts), lambda i, m: (0, i, 0)),
        ),
        out_shape=jax.ShapeDtypeStruct((parts, count, width // parts), jnp.bfloat16),
        compiler_params=params(),
        cost_estimate=cost(4 * count * width, 4 * count * width),
        name="normalise",
    )(meta, flat)


def product(x, weights):
    w0, w1, w2, wx, wy = weights
    half = wx.shape[0]
    total = nn(x(0), w0[...])
    total += nn(x(1), w1[...])
    total += nn(x(2), w2[...])
    last = x(3)
    total += nn(last[:, :half], wx[...])
    total += nn(last[:, half:], wy[...])
    return total


def kv_kernel(own_ref, sib_ref, w0, w1, w2, wx, wy, out_ref):
    step = pl.program_id(0)
    half = pl.num_programs(0) // 2
    weights = (w0, w1, w2, wx, wy)

    @pl.when(step < half)
    def _():
        out_ref[...] = product(lambda j: own_ref[j], weights).astype(jnp.bfloat16)

    @pl.when(step >= half)
    def _():
        out_ref[...] = product(lambda j: sib_ref[j], weights).astype(jnp.bfloat16)


def pair_specs(parts, block, wide, steps):
    own = pl.BlockSpec(
        (parts, block, wide), lambda i, *m: (0, jnp.minimum(i, steps // 2 - 1), 0)
    )
    sib = pl.BlockSpec((parts, block, wide), lambda i, *m: (0, jnp.maximum(i - steps // 2, 0), 0))
    return [own, sib]


def project_kv(own, sib, weights):
    parts, count, wide = own.shape
    columns = weights[0].shape[1]
    block = 256
    steps = 2 * count // block
    return pl.pallas_call(
        kv_kernel,
        grid=(steps,),
        in_specs=pair_specs(parts, block, wide, steps) + [whole()] * 5,
        out_specs=pl.BlockSpec((block, columns), lambda i: (i, 0)),
        out_shape=jax.ShapeDtypeStruct((2 * count, columns), jnp.bfloat16),
        compiler_params=params(),
        cost_estimate=cost(4 * count * parts * wide * columns, 4 * count * parts * wide),
        name="project_kv",
    )(own, sib, *weights)


def attend_kernel(factor, meta, own_ref, sib_ref, w0, w1, w2, wx, wy, kv_ref, out_ref, query):
    step = pl.program_id(0)
    half = pl.num_programs(0) // 2
    weights = (w0, w1, w2, wx, wy)

    @pl.when(step < half)
    def _():
        query[...] = product(lambda j: own_ref[j], weights).astype(jnp.bfloat16)

    @pl.when(step >= half)
    def _():
        query[...] = product(lambda j: sib_ref[j], weights).astype(jnp.bfloat16)

    length = meta[4 + step]
    start = meta[8 + step]
    positions = out_ref.shape[0]
    keys = kv_ref[:, :HD]
    values = kv_ref[:, HD:]
    row = lax.broadcasted_iota(jnp.int32, (positions, positions), 0)
    column = lax.broadcasted_iota(jnp.int32, (positions, positions), 1)
    visible = (column < length) & ((column < start) | (column <= row))
    for head in range(out_ref.shape[1] // HD):
        at = slice(head * HD, (head + 1) * HD)
        scores = jnp.where(visible, nt(query[:, at], keys) * factor, NEG)
        top = jnp.max(scores, axis=-1, keepdims=True)
        weight = jnp.where(visible, jnp.exp(scores - top), 0.0)
        weight = (weight / jnp.sum(weight, axis=-1, keepdims=True)).astype(jnp.bfloat16)
        out_ref[:, at] = nn(weight, values).astype(jnp.bfloat16)


def attend(meta, own, sib, weights, kv, positions, factor):
    parts, count, wide = own.shape
    columns = weights[0].shape[1]
    steps = 2 * count // positions
    return pl.pallas_call(
        functools.partial(attend_kernel, factor),
        grid_spec=pltpu.PrefetchScalarGridSpec(
            num_scalar_prefetch=1,
            grid=(steps,),
            in_specs=pair_specs(parts, positions, wide, steps)
            + [whole()] * 5
            + [pl.BlockSpec((positions, 2 * HD), lambda i, m: (i, 0))],
            out_specs=pl.BlockSpec((positions, columns), lambda i, m: (i, 0)),
            scratch_shapes=[pltpu.VMEM((positions, columns), jnp.bfloat16)],
        ),
        out_shape=jax.ShapeDtypeStruct((2 * count, columns), jnp.bfloat16),
        compiler_params=params(),
        cost_estimate=cost(8 * count * parts * wide * columns, 4 * count * parts * wide),
        name="attend",
    )(meta, own, sib, *weights, kv)


def expert_project_kernel(meta, own_ref, sib_ref, wq, wk, wv, wo, out_ref, cot_ref):
    step = pl.program_id(0)
    half = pl.num_programs(0) // 2

    def run(ref):
        action = ref[0]
        q, k = wq.shape[1], wk.shape[1]
        out_ref[:, :q] = nn(action, wq[...]).astype(jnp.bfloat16)
        out_ref[:, q : q + k] = nn(action, wk[...]).astype(jnp.bfloat16)
        out_ref[:, q + k :] = nn(action, wv[...]).astype(jnp.bfloat16)
        cot_ref[...] = nt(ref[1], wo[...]).astype(jnp.bfloat16)

    @pl.when(step < half)
    def _():
        run(own_ref)

    @pl.when(step >= half)
    def _():
        run(sib_ref)


def expert_project(meta, own, sib, wq, wk, wv, wo):
    _, rows, width = own.shape
    block = 256
    steps = 2 * rows // block
    q, k = wq.shape[1] // 2, wk.shape[1] // 2
    return pl.pallas_call(
        expert_project_kernel,
        grid_spec=pltpu.PrefetchScalarGridSpec(
            num_scalar_prefetch=1,
            grid=(steps,),
            in_specs=pair_specs(2, block, width, steps)
            + [
                pl.BlockSpec((width, q), lambda i, m: (0, m[1])),
                pl.BlockSpec((width, k), lambda i, m: (0, m[1])),
                pl.BlockSpec((width, k), lambda i, m: (0, m[1])),
                pl.BlockSpec((q, width), lambda i, m: (m[1], 0)),
            ],
            out_specs=[
                pl.BlockSpec((block, q + 2 * k), lambda i, m: (i, 0)),
                pl.BlockSpec((block, q), lambda i, m: (i, 0)),
            ],
        ),
        out_shape=[
            jax.ShapeDtypeStruct((2 * rows, q + 2 * k), jnp.bfloat16),
            jax.ShapeDtypeStruct((2 * rows, q), jnp.bfloat16),
        ],
        compiler_params=params(),
        cost_estimate=cost(4 * rows * width * (2 * q + 2 * k), 8 * rows * width),
        name="expert_project",
    )(meta, own, sib, wq, wk, wv, wo)


def expert_kernel(factor, spans, meta, proj_ref, dctx_ref, kv_ref, ctx_ref, grad_ref):
    step = pl.program_id(0)
    positions = meta.shape[0] and 256
    width = dctx_ref.shape[1]
    heads = width // HD
    rows = heads * PAD
    own_column = lax.broadcasted_iota(jnp.int32, (rows, PAD), 1)
    pre_column = lax.broadcasted_iota(jnp.int32, (rows, positions), 1)
    for s in range(spans):
        sample = meta[12 + step * spans + s]
        valid = pre_column < meta[4 + sample]
        own_valid = own_column < STEPS
        at = slice(s * PAD, (s + 1) * PAD)
        base = pl.multiple_of(sample * positions, positions)
        pre_keys = kv_ref[pl.ds(base, positions), :HD]
        pre_values = kv_ref[pl.ds(base, positions), HD:]
        stack = lambda ref: jnp.concatenate(
            [ref[at, h * HD : (h + 1) * HD] for h in range(heads)], axis=0
        )
        query = stack(proj_ref)
        cot = stack(dctx_ref)
        own_keys = proj_ref[at, width : width + HD]
        own_values = proj_ref[at, width + HD :]
        score_pre = jnp.where(valid, nt(query, pre_keys) * factor, NEG)
        score_own = jnp.where(own_valid, nt(query, own_keys) * factor, NEG)
        peak = jnp.maximum(
            jnp.max(score_pre, axis=-1, keepdims=True), jnp.max(score_own, axis=-1, keepdims=True)
        )
        exp_pre = jnp.where(valid, jnp.exp(score_pre - peak), 0.0)
        exp_own = jnp.where(own_valid, jnp.exp(score_own - peak), 0.0)
        total = jnp.sum(exp_pre, axis=-1, keepdims=True) + jnp.sum(exp_own, axis=-1, keepdims=True)
        prob_pre = exp_pre / total
        prob_own = exp_own / total
        half_pre = prob_pre.astype(jnp.bfloat16)
        half_own = prob_own.astype(jnp.bfloat16)
        context = (nn(half_pre, pre_values) + nn(half_own, own_values)).astype(jnp.bfloat16)
        dprob_pre = nt(cot, pre_values)
        dprob_own = nt(cot, own_values)
        delta = jnp.sum(prob_pre * dprob_pre, axis=-1, keepdims=True) + jnp.sum(
            prob_own * dprob_own, axis=-1, keepdims=True
        )
        dscore_pre = (prob_pre * (dprob_pre - delta) * factor).astype(jnp.bfloat16)
        dscore_own = (prob_own * (dprob_own - delta) * factor).astype(jnp.bfloat16)
        dquery = (nn(dscore_pre, pre_keys) + nn(dscore_own, own_keys)).astype(jnp.bfloat16)
        for h in range(heads):
            part = slice(h * PAD, (h + 1) * PAD)
            ctx_ref[at, h * HD : (h + 1) * HD] = context[part]
            grad_ref[at, h * HD : (h + 1) * HD] = dquery[part]
        grad_ref[at, width : width + HD] = tn(dscore_own, query).astype(jnp.bfloat16)
        grad_ref[at, width + HD :] = tn(half_own, cot).astype(jnp.bfloat16)


def expert_attend(meta, proj, dctx, kv, factor):
    rows, columns = proj.shape
    width = dctx.shape[1]
    spans = 4
    steps = rows // (PAD * spans)
    block = PAD * spans
    return pl.pallas_call(
        functools.partial(expert_kernel, factor, spans),
        grid_spec=pltpu.PrefetchScalarGridSpec(
            num_scalar_prefetch=1,
            grid=(steps,),
            in_specs=[
                pl.BlockSpec((block, columns), lambda i, m: (i, 0)),
                pl.BlockSpec((block, width), lambda i, m: (i, 0)),
                whole(),
            ],
            out_specs=[
                pl.BlockSpec((block, width), lambda i, m: (i, 0)),
                pl.BlockSpec((block, columns), lambda i, m: (i, 0)),
            ],
        ),
        out_shape=[
            jax.ShapeDtypeStruct((rows, width), jnp.bfloat16),
            jax.ShapeDtypeStruct((rows, columns), jnp.bfloat16),
        ],
        compiler_params=params(),
        cost_estimate=cost(40 * rows * 320 * width, 8 * rows * columns),
        name="expert_attend",
    )(meta, proj, dctx, kv)


def grads_kernel(meta, own_ref, sib_ref, ctx_ref, grad_ref, ax_ref, ak_ref, by_ref, bk_ref):
    chip = meta[0]
    step = pl.program_id(0)
    rows = own_ref.shape[1]
    tall = ax_ref.shape[1]
    wide = grad_ref.shape[1]
    heads = ctx_ref.shape[1] // HD

    def piece(route, j, ref):
        at = pl.ds(pl.multiple_of((route * 4 + (chip ^ j)) * tall, tall), tall)
        ref[0, :, :wide] = tn(own_ref[0, :, at], grad_ref[:rows]) + tn(
            sib_ref[0, :, at], grad_ref[rows:]
        )
        for h in range(heads):
            cut = slice(h * HD, (h + 1) * HD)
            ref[0, :, wide + h * tall : wide + (h + 1) * tall] = tn(
                ctx_ref[:rows, cut], own_ref[1, :, at]
            ) + tn(ctx_ref[rows:, cut], sib_ref[1, :, at])

    piece(0, 1 + 2 * step, ax_ref)
    piece(1, 2 + step, by_ref)
    piece(0, 2 * step, ak_ref)
    piece(1, step, bk_ref)


def weight_grads(meta, own, sib, ctx, grad):
    _, rows, width = own.shape
    tall = width // 8
    columns = grad.shape[1] + ctx.shape[1] // HD * tall
    out = jax.ShapeDtypeStruct((2, tall, columns), jnp.float32)
    return pl.pallas_call(
        grads_kernel,
        grid_spec=pltpu.PrefetchScalarGridSpec(
            num_scalar_prefetch=1,
            grid=(2,),
            in_specs=[whole()] * 4,
            out_specs=[pl.BlockSpec((1, tall, columns), lambda i, m: (i, 0, 0))] * 4,
        ),
        out_shape=[out] * 4,
        compiler_params=params(),
        cost_estimate=cost(4 * rows * width * columns, 16 * width * columns),
        name="weight_grads",
    )(meta, own, sib, ctx, grad)


def place_kernel(meta, *refs):
    own, sib, outs = refs[:5], refs[5:10], refs[10:]
    step = pl.program_id(0)
    first = meta[1] == 0
    wq, wk, wv, wo = outs
    tall = wq.shape[0]
    q, k = wq.shape[1] // 2, wk.shape[1] // 2
    heads = wo.shape[0] // (2 * HD)

    def pick(group, route, j):
        if j < 3:
            return group[j][route]
        return group[3 + route][...]

    for route in range(2):
        for j in range(4):

            @pl.when(step == route * 4 + j)
            def _():
                mine, other = pick(own, route, j), pick(sib, route, j)
                for side, block in enumerate(
                    (jnp.where(first, mine, other), jnp.where(first, other, mine))
                ):
                    wq[:, side * q : (side + 1) * q] = block[:, :q]
                    wk[:, side * k : (side + 1) * k] = block[:, q : q + k]
                    wv[:, side * k : (side + 1) * k] = block[:, q + k : q + 2 * k]
                    for h in range(heads):
                        row = (side * heads + h) * HD
                        cut = q + 2 * k + h * tall
                        wo[row : row + HD] = block[:, cut : cut + tall]


def place_grads(meta, own, sib, shapes):
    tall = own[0].shape[1]

    def spot(i, m):
        return (i // 4) * 4 + (m[0] ^ (i % 4))

    rows = lambda s: pl.BlockSpec((tall, s[1]), lambda i, m: (spot(i, m), 0))
    specs = [rows(s) for s in shapes[:3]]
    specs.append(pl.BlockSpec((shapes[3][0], tall), lambda i, m: (0, spot(i, m))))
    return pl.pallas_call(
        place_kernel,
        grid_spec=pltpu.PrefetchScalarGridSpec(
            num_scalar_prefetch=1,
            grid=(8,),
            in_specs=[whole()] * 10,
            out_specs=specs,
        ),
        out_shape=[jax.ShapeDtypeStruct(s, jnp.float32) for s in shapes],
        compiler_params=params(),
        cost_estimate=cost(0, 2 * 4 * sum(s[0] * s[1] for s in shapes)),
        name="place_grads",
    )(meta, *own, *sib)


def output_kernel(meta, tok_ref, mid, u1, u2, u3, d1, d2, d3, *refs):
    wos, out_ref, ctx = refs[:10], refs[10], refs[11]
    chip, plane = meta[0], meta[2]
    step = pl.program_id(0)
    quarter = wos[0].shape[1]

    @pl.when(step == 0)
    def _():
        ctx[plane] = mid[...]
        for k, (up, down) in enumerate(((u1, d1), (u2, d2), (u3, d3)), 1):

            @pl.when(plane >= k)
            def _():
                ctx[plane - k] = up[...]

            @pl.when(plane + k <= 3)
            def _():
                ctx[plane + k] = down[...]

    def run(group):
        total = tok_ref[...].astype(jnp.float32)
        for j in range(4):
            column = pl.multiple_of((chip ^ j) * quarter, quarter)
            for r in range(4):
                source = (chip ^ j) ^ plane ^ r
                if j < 3:
                    weight = group[j][r]
                else:
                    weight = group[3 + r // 2][r % 2]
                total += nn(ctx[source, :, pl.ds(column, quarter)], weight)
        out_ref[...] = total.astype(jnp.bfloat16)

    @pl.when(step == 0)
    def _():
        run(wos[:5])

    @pl.when(step == 1)
    def _():
        run(wos[5:])


def output(meta, flat, contexts, own, sib):
    count = flat.shape[0]
    half = own[0].shape[2]
    wide = contexts[0].shape[1]
    return pl.pallas_call(
        output_kernel,
        grid_spec=pltpu.PrefetchScalarGridSpec(
            num_scalar_prefetch=1,
            grid=(2,),
            in_specs=[pl.BlockSpec((count, half), lambda i, m: (0, 2 * m[2] + (m[1] ^ i)))]
            + [whole()] * 17,
            out_specs=pl.BlockSpec((count, half), lambda i, m: (0, m[1] ^ i)),
            scratch_shapes=[pltpu.VMEM((4, count, wide), jnp.bfloat16)],
        ),
        out_shape=jax.ShapeDtypeStruct((count, 2 * half), jnp.bfloat16),
        compiler_params=params(),
        cost_estimate=cost(16 * count * wide * half, 32 * wide * half),
        name="output",
    )(meta, flat, *contexts, *own, *sib)


def plane_body(
    prefix_tokens,
    prefix_len,
    causal_start,
    span_sample,
    bb_wq,
    bb_wk,
    bb_wv,
    bb_wo,
    action_tokens,
    ex_wq,
    ex_wk,
    ex_wv,
    ex_wo,
    action_cot,
):
    samples, positions, width = prefix_tokens.shape
    factor = 1.0 / math.sqrt(HD)
    count = samples * positions
    flat = prefix_tokens.reshape(count, width)
    device = lax.axis_index("dp")
    chip, core = device // 2, device % 2
    plane = lax.axis_index("tensor")

    def across(mask):
        return lambda x: lax.ppermute(x, "dp", [(i, i ^ mask) for i in range(8)])

    swap, over_x, over_y = across(1), across(2), across(4)

    def spread(x):
        from_x, from_y = over_x(x), over_y(x)
        half = x.shape[0] // 2
        return x, from_x, from_y, over_x(from_y[:half]), over_y(from_x[half:])

    local = jnp.concatenate([prefix_len, causal_start, span_sample])
    remote = swap(local)
    meta = jnp.concatenate(
        [
            jnp.stack([chip, core, plane, 0]).astype(jnp.int32),
            local[:2],
            remote[:2],
            local[2:4],
            remote[2:4],
            local[4:],
            remote[4:] + samples,
        ]
    )
    chip_meta = jnp.stack([chip, core, plane, 0]).astype(jnp.int32)

    def halves(weight):
        size = weight.shape[1] // 2
        mine = lax.dynamic_slice_in_dim(weight, core * size, size, 1)
        other = lax.dynamic_slice_in_dim(weight, (1 - core) * size, size, 1)
        return mine, other

    def joined(mine, got):
        return jnp.where(
            core == 0, jnp.concatenate([mine, got]), jnp.concatenate([got, mine])
        )

    k_mine, k_other = halves(bb_wk)
    v_mine, v_other = halves(bb_wv)
    kv_got = swap(jnp.concatenate([k_other, v_other], axis=1))
    kv_shard = joined(jnp.concatenate([k_mine, v_mine], axis=1), kv_got)
    q_mine, q_other = halves(bb_wq)
    q_shard = joined(q_mine, swap(q_other))
    kv_weights = spread(kv_shard)
    q_weights = spread(q_shard)

    normed = normalise(chip_meta, flat, 4)
    normed_sib = swap(normed)

    spans = action_tokens.shape[0]
    pad = ((0, 0), (0, PAD - STEPS), (0, 0))
    pair = jnp.stack([jnp.pad(action_tokens, pad), jnp.pad(action_cot, pad)])
    pair = pair.reshape(2, spans * PAD, action_tokens.shape[2])
    pair_sib = swap(pair)
    proj, dctx = expert_project(chip_meta, pair, pair_sib, ex_wq, ex_wk, ex_wv, ex_wo)

    kv = project_kv(normed, normed_sib, kv_weights)
    ectx, egrad = expert_attend(meta, proj, dctx, kv, factor)
    ax, ak, by, bk = weight_grads(chip_meta, pair, pair_sib, ectx, egrad)
    a_sum = ak + over_x(ax)
    b_sum = bk + over_y(by)
    mine = jnp.stack([a_sum[0] + over_y(a_sum[1]), b_sum[0] + over_x(b_sum[1])])
    from_x, from_y = over_x(mine), over_y(mine)
    full = (mine, from_x, from_y, over_x(from_y[0]), over_y(from_x[1]))
    full_sib = tuple(swap(x) for x in full)
    shapes = (ex_wq.shape, ex_wk.shape, ex_wv.shape, ex_wo.shape)
    grads = place_grads(chip_meta, full, full_sib, shapes)

    quarter = bb_wo.shape[0] // 4
    got = []
    for r in range(4):
        to = chip ^ plane ^ r
        perm = [
            (((a * 2 + k) * 4 + z), (((a ^ z ^ r) * 2 + k) * 4 + a))
            for a in range(4)
            for k in range(2)
            for z in range(4)
        ]
        piece = lax.dynamic_slice_in_dim(bb_wo, to * quarter, quarter, 0)
        got.append(lax.ppermute(piece, ("dp", "tensor"), perm))
    wo_own = spread(jnp.stack(got))
    wo_sib = tuple(swap(x) for x in wo_own)

    ctx = attend(meta, normed, normed_sib, q_weights, kv, positions, factor)
    ctx_own, ctx_other = ctx[:count], ctx[count:]
    ctx_got = swap(ctx_other)
    ctx_rows = jnp.where(
        core == 0,
        jnp.concatenate([ctx_own, ctx_got], axis=1),
        jnp.concatenate([ctx_got, ctx_own], axis=1),
    )
    up = lambda x: lax.ppermute(x, "tensor", [(0, 1), (1, 2), (2, 3)])
    down = lambda x: lax.ppermute(x, "tensor", [(3, 2), (2, 1), (1, 0)])
    u1, d1 = up(ctx_rows), down(ctx_rows)
    u2, d2 = up(u1), down(d1)
    u3, d3 = up(u2), down(d2)
    out = output(chip_meta, flat, (ctx_rows, u1, u2, u3, d1, d2, d3), wo_own, wo_sib)
    return (out.reshape(samples, positions, -1), *grads)


def fits_plane(mesh):
    return mesh.shape["dp"] == 8 and mesh.shape["tensor"] == 4


def solution(mesh):
    in_specs = (
        P("dp", None, None),
        P("dp"),
        P("dp"),
        P("dp"),
        P("dp", "tensor"),
        P("dp", "tensor"),
        P("dp", "tensor"),
        P("tensor", "dp"),
        P("dp", None, None),
        P(None, "tensor"),
        P(None, "tensor"),
        P(None, "tensor"),
        P("tensor", None),
        P("dp", None, None),
    )
    out_specs = (
        P("dp", None, "tensor"),
        P(None, "tensor"),
        P(None, "tensor"),
        P(None, "tensor"),
        P("tensor", None),
    )
    body = plane_body if fits_plane(mesh) else general_body
    return jax.shard_map(body, mesh=mesh, in_specs=in_specs, out_specs=out_specs, check_vma=False)
```

```python
import functools
import math

import jax
import jax.numpy as jnp
from jax import lax
from jax.experimental import pallas as pl
from jax.experimental.pallas import tpu as pltpu
from jax.sharding import PartitionSpec as P

HD = 128
STEPS = 50


def general_body(
    prefix_tokens,
    prefix_len,
    causal_start,
    span_sample,
    bb_wq,
    bb_wk,
    bb_wv,
    bb_wo,
    action_tokens,
    ex_wq,
    ex_wk,
    ex_wv,
    ex_wo,
    action_cot,
):
    samples, positions, width = prefix_tokens.shape
    factor = 1.0 / math.sqrt(HD)
    kv_local = bb_wk.shape[1] // HD
    group = bb_wq.shape[1] // bb_wk.shape[1]
    egroup = ex_wq.shape[1] // ex_wk.shape[1]
    count = samples * positions
    flat = prefix_tokens.reshape(count, width)
    widened = flat.astype(jnp.float32)
    normed = (
        widened * lax.rsqrt(jnp.mean(widened * widened, axis=-1, keepdims=True) + 1e-06)
    ).astype(jnp.bfloat16)
    pieces = (
        lax.all_gather(bb_wq, "dp", axis=0, tiled=True),
        lax.all_gather(bb_wk, "dp", axis=0, tiled=True),
        lax.all_gather(bb_wv, "dp", axis=0, tiled=True),
    )
    query_sum, key_sum, value_sum = tuple(
        (jnp.dot(normed, piece, preferred_element_type=jnp.float32) for piece in pieces)
    )
    query = query_sum.astype(jnp.bfloat16).reshape(samples, positions, kv_local, group, HD)
    keys = key_sum.astype(jnp.bfloat16).reshape(samples, positions, kv_local, HD)
    values = value_sum.astype(jnp.bfloat16).reshape(samples, positions, kv_local, HD)
    scores = (
        jnp.einsum("sigeh,sjgh->sgeij", query, keys, preferred_element_type=jnp.float32) * factor
    )
    places = jnp.arange(positions, dtype=jnp.int32)
    length_view = prefix_len[:, None, None, None, None]
    start_view = causal_start[:, None, None, None, None]
    visible = (places[None, None, None, None, :] < length_view) & (
        (places[None, None, None, None, :] < start_view)
        | (places[None, None, None, None, :] <= places[None, None, None, :, None])
    )
    scores = jnp.where(visible, scores, -1e30)
    top = jnp.max(scores, axis=-1, keepdims=True)
    weights = jnp.where(visible, jnp.exp(scores - top), 0.0)
    weights = (weights / jnp.sum(weights, axis=-1, keepdims=True)).astype(jnp.bfloat16)
    context = (
        jnp.einsum("sgeij,sjgh->sigeh", weights, values, preferred_element_type=jnp.float32)
        .astype(jnp.bfloat16)
        .reshape(count, bb_wq.shape[1])
    )
    partial_out = jnp.dot(
        context, lax.all_gather(bb_wo, "dp", axis=1, tiled=True), preferred_element_type=jnp.float32
    )
    summed = lax.psum_scatter(partial_out, "tensor", scatter_dimension=1, tiled=True)
    share = summed.shape[1]
    residual = lax.dynamic_slice_in_dim(widened, lax.axis_index("tensor") * share, share, 1)
    prefix_out = (residual + summed).astype(jnp.bfloat16).reshape(samples, positions, share)
    spans = action_tokens.shape[0]
    rows = spans * STEPS
    action_flat = action_tokens.reshape(rows, action_tokens.shape[2])
    cot_flat = action_cot.reshape(rows, action_cot.shape[2])
    pre_keys = jnp.take(keys, span_sample, axis=0)
    pre_values = jnp.take(values, span_sample, axis=0)
    span_length = jnp.take(prefix_len, span_sample, axis=0)
    equery = (
        jnp.dot(action_flat, ex_wq, preferred_element_type=jnp.float32)
        .astype(jnp.bfloat16)
        .reshape(spans, STEPS, kv_local, egroup, HD)
    )
    own_keys = (
        jnp.dot(action_flat, ex_wk, preferred_element_type=jnp.float32)
        .astype(jnp.bfloat16)
        .reshape(spans, STEPS, kv_local, HD)
    )
    own_values = (
        jnp.dot(action_flat, ex_wv, preferred_element_type=jnp.float32)
        .astype(jnp.bfloat16)
        .reshape(spans, STEPS, kv_local, HD)
    )
    valid = (places[None, :] < span_length[:, None])[:, None, None, None, :]
    score_pre = (
        jnp.einsum("ctgeh,cpgh->cgetp", equery, pre_keys, preferred_element_type=jnp.float32)
        * factor
    )
    score_pre = jnp.where(valid, score_pre, -1e30)
    score_own = (
        jnp.einsum("ctgeh,cugh->cgetu", equery, own_keys, preferred_element_type=jnp.float32)
        * factor
    )
    peak = jnp.maximum(jnp.max(score_pre, axis=-1), jnp.max(score_own, axis=-1))[..., None]
    exp_pre = jnp.where(valid, jnp.exp(score_pre - peak), 0.0)
    exp_own = jnp.exp(score_own - peak)
    total = jnp.sum(exp_pre, axis=-1, keepdims=True) + jnp.sum(exp_own, axis=-1, keepdims=True)
    prob_pre = exp_pre / total
    prob_own = exp_own / total
    half_pre = prob_pre.astype(jnp.bfloat16)
    half_own = prob_own.astype(jnp.bfloat16)
    econtext = (
        jnp.einsum("cgetp,cpgh->ctgeh", half_pre, pre_values, preferred_element_type=jnp.float32)
        + jnp.einsum("cgetu,cugh->ctgeh", half_own, own_values, preferred_element_type=jnp.float32)
    ).astype(jnp.bfloat16)
    econtext_flat = econtext.reshape(rows, ex_wq.shape[1])
    grad_out_local = jnp.einsum(
        "ti,tj->ij", econtext_flat, cot_flat, preferred_element_type=jnp.float32
    )
    dcontext = (
        jnp.einsum("tj,ij->ti", cot_flat, ex_wo, preferred_element_type=jnp.float32)
        .astype(jnp.bfloat16)
        .reshape(spans, STEPS, kv_local, egroup, HD)
    )
    dprob_pre = jnp.einsum(
        "ctgeh,cpgh->cgetp", dcontext, pre_values, preferred_element_type=jnp.float32
    )
    dprob_own = jnp.einsum(
        "ctgeh,cugh->cgetu", dcontext, own_values, preferred_element_type=jnp.float32
    )
    delta = (jnp.sum(prob_pre * dprob_pre, axis=-1) + jnp.sum(prob_own * dprob_own, axis=-1))[
        ..., None
    ]
    dscore_pre = (prob_pre * (dprob_pre - delta) * factor).astype(jnp.bfloat16)
    dscore_own = (prob_own * (dprob_own - delta) * factor).astype(jnp.bfloat16)
    dquery = (
        jnp.einsum("cgetp,cpgh->ctgeh", dscore_pre, pre_keys, preferred_element_type=jnp.float32)
        + jnp.einsum("cgetu,cugh->ctgeh", dscore_own, own_keys, preferred_element_type=jnp.float32)
    ).astype(jnp.bfloat16)
    dkeys = jnp.einsum(
        "cgetu,ctgeh->cugh", dscore_own, equery, preferred_element_type=jnp.float32
    ).astype(jnp.bfloat16)
    dvalues = jnp.einsum(
        "cgetu,ctgeh->cugh", half_own, dcontext, preferred_element_type=jnp.float32
    ).astype(jnp.bfloat16)
    grad_query_local = jnp.einsum(
        "ti,tj->ij",
        action_flat,
        dquery.reshape(rows, ex_wq.shape[1]),
        preferred_element_type=jnp.float32,
    )
    grad_key_local = jnp.einsum(
        "ti,tj->ij",
        action_flat,
        dkeys.reshape(rows, ex_wk.shape[1]),
        preferred_element_type=jnp.float32,
    )
    grad_value_local = jnp.einsum(
        "ti,tj->ij",
        action_flat,
        dvalues.reshape(rows, ex_wv.shape[1]),
        preferred_element_type=jnp.float32,
    )
    grad_wq, grad_wk, grad_wv, grad_wo = lax.psum(
        (grad_query_local, grad_key_local, grad_value_local, grad_out_local), "dp"
    )
    return (prefix_out, grad_wq, grad_wk, grad_wv, grad_wo)


NEG = -1e30
PAD = 64
HIGH = 56 * 1024 * 1024


def params():
    return pltpu.CompilerParams(vmem_limit_bytes=HIGH)


def cost(flops, moved):
    return pl.CostEstimate(flops=int(flops), bytes_accessed=int(moved), transcendentals=0)


def whole():
    return pl.BlockSpec(memory_space=pltpu.VMEM)


def nt(a, b):
    return lax.dot_general(a, b, (((1,), (1,)), ((), ())), preferred_element_type=jnp.float32)


def tn(a, b):
    return lax.dot_general(a, b, (((0,), (0,)), ((), ())), preferred_element_type=jnp.float32)


def nn(a, b):
    return jnp.dot(a, b, preferred_element_type=jnp.float32)


def norm_kernel(meta, x_ref, out_ref):
    chip, core = meta[0], meta[1]
    parts, rows, wide = out_ref.shape
    half = wide // 2
    x = x_ref[...].astype(jnp.float32)
    scale = lax.rsqrt(jnp.mean(x * x, axis=-1, keepdims=True) + 1e-06)
    for j in range(parts):
        for side in range(2):
            at = pl.multiple_of(((chip ^ j) * 2 + (core ^ side)) * half, half)
            piece = x_ref[:, pl.ds(at, half)].astype(jnp.float32)
            out_ref[j, :, side * half : (side + 1) * half] = (piece * scale).astype(jnp.bfloat16)


def normalise(meta, flat, parts):
    count, width = flat.shape
    block = 128
    return pl.pallas_call(
        norm_kernel,
        grid_spec=pltpu.PrefetchScalarGridSpec(
            num_scalar_prefetch=1,
            grid=(count // block,),
            in_specs=[pl.BlockSpec((block, width), lambda i, m: (i, 0))],
            out_specs=pl.BlockSpec((parts, block, width // parts), lambda i, m: (0, i, 0)),
        ),
        out_shape=jax.ShapeDtypeStruct((parts, count, width // parts), jnp.bfloat16),
        compiler_params=params(),
        cost_estimate=cost(4 * count * width, 4 * count * width),
        name="normalise",
    )(meta, flat)


def product(ref, weights, swapped):
    w0, w1, w2, wx, wy = weights
    half = wx.shape[0]
    first, second = slice(0, half), slice(half, 2 * half)
    if not swapped:
        total = nn(ref[0], w0[...]) + nn(ref[1], w1[...]) + nn(ref[2], w2[...])
        return total + nn(ref[3, :, first], wx[...]) + nn(ref[3, :, second], wy[...])
    total = nn(ref[3, :, second], wx[...]) + nn(ref[3, :, first], wy[...])
    for j, weight in enumerate((w0, w1, w2)):
        total += nn(ref[j, :, second], weight[first]) + nn(ref[j, :, first], weight[second])
    return total


def kv_kernel(own_ref, sib_ref, w0, w1, w2, wx, wy, out_ref):
    step = pl.program_id(0)
    half = pl.num_programs(0) // 2
    weights = (w0, w1, w2, wx, wy)

    @pl.when(step < half)
    def _():
        out_ref[...] = product(own_ref, weights, False).astype(jnp.bfloat16)

    @pl.when(step >= half)
    def _():
        out_ref[...] = product(sib_ref, weights, True).astype(jnp.bfloat16)


def pair_specs(parts, block, wide, steps, sib_first=False):
    first = pl.BlockSpec(
        (parts, block, wide), lambda i, *m: (0, jnp.minimum(i, steps // 2 - 1), 0)
    )
    then = pl.BlockSpec((parts, block, wide), lambda i, *m: (0, jnp.maximum(i - steps // 2, 0), 0))
    return [then, first] if sib_first else [first, then]


def project_kv(own, sib, weights):
    parts, count, wide = own.shape
    columns = weights[0].shape[1]
    block = 256
    steps = 2 * count // block
    return pl.pallas_call(
        kv_kernel,
        grid=(steps,),
        in_specs=pair_specs(parts, block, wide, steps) + [whole()] * 5,
        out_specs=pl.BlockSpec((block, columns), lambda i: (i, 0)),
        out_shape=jax.ShapeDtypeStruct((2 * count, columns), jnp.bfloat16),
        compiler_params=params(),
        cost_estimate=cost(4 * count * parts * wide * columns, 4 * count * parts * wide),
        name="project_kv",
    )(own, sib, *weights)


def attend_kernel(factor, meta, own_ref, sib_ref, w0, w1, w2, wx, wy, kv_ref, own_out, sib_out, query, context):
    step = pl.program_id(0)
    half = pl.num_programs(0) // 2
    weights = (w0, w1, w2, wx, wy)

    @pl.when(step >= half)
    def _():
        query[...] = product(own_ref, weights, False).astype(jnp.bfloat16)

    @pl.when(step < half)
    def _():
        query[...] = product(sib_ref, weights, True).astype(jnp.bfloat16)

    sample = lax.rem(step + half, 2 * half)
    length = meta[4 + sample]
    start = meta[8 + sample]
    positions = context.shape[0]
    keys = kv_ref[:, :HD]
    values = kv_ref[:, HD:]
    row = lax.broadcasted_iota(jnp.int32, (positions, positions), 0)
    column = lax.broadcasted_iota(jnp.int32, (positions, positions), 1)
    visible = (column < length) & ((column < start) | (column <= row))
    for head in range(context.shape[1] // HD):
        at = slice(head * HD, (head + 1) * HD)
        scores = jnp.where(visible, nt(query[:, at], keys) * factor, NEG)
        top = jnp.max(scores, axis=-1, keepdims=True)
        weight = jnp.where(visible, jnp.exp(scores - top), 0.0)
        weight = (weight / jnp.sum(weight, axis=-1, keepdims=True)).astype(jnp.bfloat16)
        context[:, at] = nn(weight, values).astype(jnp.bfloat16)

    @pl.when(step >= half)
    def _():
        own_out[...] = context[...]

    @pl.when(step < half)
    def _():
        sib_out[...] = context[...]


def attend(meta, own, sib, weights, kv, positions, factor):
    parts, count, wide = own.shape
    columns = weights[0].shape[1]
    steps = 2 * count // positions
    half = steps // 2
    out = jax.ShapeDtypeStruct((count, columns), jnp.bfloat16)
    return pl.pallas_call(
        functools.partial(attend_kernel, factor),
        grid_spec=pltpu.PrefetchScalarGridSpec(
            num_scalar_prefetch=1,
            grid=(steps,),
            in_specs=pair_specs(parts, positions, wide, steps, True)
            + [whole()] * 5
            + [pl.BlockSpec((positions, 2 * HD), lambda i, m: ((i + half) % steps, 0))],
            out_specs=[
                pl.BlockSpec((positions, columns), lambda i, m: (jnp.maximum(i - half, 0), 0)),
                pl.BlockSpec((positions, columns), lambda i, m: (jnp.minimum(i, half - 1), 0)),
            ],
            scratch_shapes=[pltpu.VMEM((positions, columns), jnp.bfloat16)] * 2,
        ),
        out_shape=[out, out],
        compiler_params=params(),
        cost_estimate=cost(8 * count * parts * wide * columns, 4 * count * parts * wide),
        name="attend",
    )(meta, own, sib, *weights, kv)


def expert_project_kernel(meta, own_ref, sib_ref, wq, wk, wv, wo, out_ref, cot_ref):
    step = pl.program_id(0)
    half = pl.num_programs(0) // 2

    def run(ref):
        action = ref[0]
        q, k = wq.shape[1], wk.shape[1]
        out_ref[:, :q] = nn(action, wq[...]).astype(jnp.bfloat16)
        out_ref[:, q : q + k] = nn(action, wk[...]).astype(jnp.bfloat16)
        out_ref[:, q + k :] = nn(action, wv[...]).astype(jnp.bfloat16)
        cot_ref[...] = nt(ref[1], wo[...]).astype(jnp.bfloat16)

    @pl.when(step < half)
    def _():
        run(own_ref)

    @pl.when(step >= half)
    def _():
        run(sib_ref)


def expert_project(meta, own, sib, wq, wk, wv, wo):
    _, rows, width = own.shape
    block = 256
    steps = 2 * rows // block
    q, k = wq.shape[1] // 2, wk.shape[1] // 2
    return pl.pallas_call(
        expert_project_kernel,
        grid_spec=pltpu.PrefetchScalarGridSpec(
            num_scalar_prefetch=1,
            grid=(steps,),
            in_specs=pair_specs(2, block, width, steps)
            + [
                pl.BlockSpec((width, q), lambda i, m: (0, m[1])),
                pl.BlockSpec((width, k), lambda i, m: (0, m[1])),
                pl.BlockSpec((width, k), lambda i, m: (0, m[1])),
                pl.BlockSpec((q, width), lambda i, m: (m[1], 0)),
            ],
            out_specs=[
                pl.BlockSpec((block, q + 2 * k), lambda i, m: (i, 0)),
                pl.BlockSpec((block, q), lambda i, m: (i, 0)),
            ],
        ),
        out_shape=[
            jax.ShapeDtypeStruct((2 * rows, q + 2 * k), jnp.bfloat16),
            jax.ShapeDtypeStruct((2 * rows, q), jnp.bfloat16),
        ],
        compiler_params=params(),
        cost_estimate=cost(4 * rows * width * (2 * q + 2 * k), 8 * rows * width),
        name="expert_project",
    )(meta, own, sib, wq, wk, wv, wo)


def expert_kernel(factor, spans, meta, proj_ref, dctx_ref, kv_ref, ctx_ref, grad_ref):
    step = pl.program_id(0)
    positions = meta.shape[0] and 256
    width = dctx_ref.shape[1]
    heads = width // HD
    rows = heads * PAD
    own_column = lax.broadcasted_iota(jnp.int32, (rows, PAD), 1)
    pre_column = lax.broadcasted_iota(jnp.int32, (rows, positions), 1)
    for s in range(spans):
        sample = meta[12 + step * spans + s]
        valid = pre_column < meta[4 + sample]
        own_valid = own_column < STEPS
        at = slice(s * PAD, (s + 1) * PAD)
        base = pl.multiple_of(sample * positions, positions)
        pre_keys = kv_ref[pl.ds(base, positions), :HD]
        pre_values = kv_ref[pl.ds(base, positions), HD:]
        stack = lambda ref: jnp.concatenate(
            [ref[at, h * HD : (h + 1) * HD] for h in range(heads)], axis=0
        )
        query = stack(proj_ref)
        cot = stack(dctx_ref)
        own_keys = proj_ref[at, width : width + HD]
        own_values = proj_ref[at, width + HD :]
        score_pre = jnp.where(valid, nt(query, pre_keys) * factor, NEG)
        score_own = jnp.where(own_valid, nt(query, own_keys) * factor, NEG)
        peak = jnp.maximum(
            jnp.max(score_pre, axis=-1, keepdims=True), jnp.max(score_own, axis=-1, keepdims=True)
        )
        exp_pre = jnp.where(valid, jnp.exp(score_pre - peak), 0.0)
        exp_own = jnp.where(own_valid, jnp.exp(score_own - peak), 0.0)
        total = jnp.sum(exp_pre, axis=-1, keepdims=True) + jnp.sum(exp_own, axis=-1, keepdims=True)
        prob_pre = exp_pre / total
        prob_own = exp_own / total
        half_pre = prob_pre.astype(jnp.bfloat16)
        half_own = prob_own.astype(jnp.bfloat16)
        context = (nn(half_pre, pre_values) + nn(half_own, own_values)).astype(jnp.bfloat16)
        dprob_pre = nt(cot, pre_values)
        dprob_own = nt(cot, own_values)
        delta = jnp.sum(prob_pre * dprob_pre, axis=-1, keepdims=True) + jnp.sum(
            prob_own * dprob_own, axis=-1, keepdims=True
        )
        dscore_pre = (prob_pre * (dprob_pre - delta) * factor).astype(jnp.bfloat16)
        dscore_own = (prob_own * (dprob_own - delta) * factor).astype(jnp.bfloat16)
        dquery = (nn(dscore_pre, pre_keys) + nn(dscore_own, own_keys)).astype(jnp.bfloat16)
        for h in range(heads):
            part = slice(h * PAD, (h + 1) * PAD)
            ctx_ref[at, h * HD : (h + 1) * HD] = context[part]
            grad_ref[at, h * HD : (h + 1) * HD] = dquery[part]
        grad_ref[at, width : width + HD] = tn(dscore_own, query).astype(jnp.bfloat16)
        grad_ref[at, width + HD :] = tn(half_own, cot).astype(jnp.bfloat16)


def expert_attend(meta, proj, dctx, kv, factor):
    rows, columns = proj.shape
    width = dctx.shape[1]
    spans = 4
    steps = rows // (PAD * spans)
    block = PAD * spans
    return pl.pallas_call(
        functools.partial(expert_kernel, factor, spans),
        grid_spec=pltpu.PrefetchScalarGridSpec(
            num_scalar_prefetch=1,
            grid=(steps,),
            in_specs=[
                pl.BlockSpec((block, columns), lambda i, m: (i, 0)),
                pl.BlockSpec((block, width), lambda i, m: (i, 0)),
                whole(),
            ],
            out_specs=[
                pl.BlockSpec((block, width), lambda i, m: (i, 0)),
                pl.BlockSpec((block, columns), lambda i, m: (i, 0)),
            ],
        ),
        out_shape=[
            jax.ShapeDtypeStruct((rows, width), jnp.bfloat16),
            jax.ShapeDtypeStruct((rows, columns), jnp.bfloat16),
        ],
        compiler_params=params(),
        cost_estimate=cost(40 * rows * 320 * width, 8 * rows * columns),
        name="expert_attend",
    )(meta, proj, dctx, kv)


def grads_kernel(meta, own_ref, sib_ref, ctx_ref, grad_ref, ax_ref, ak_ref, by_ref, bk_ref):
    chip = meta[0]
    step = pl.program_id(0)
    rows = own_ref.shape[1]
    tall = ax_ref.shape[1]
    wide = grad_ref.shape[1]
    heads = ctx_ref.shape[1] // HD

    def piece(route, j, ref):
        at = pl.ds(pl.multiple_of((route * 4 + (chip ^ j)) * tall, tall), tall)
        ref[0, :, :wide] = tn(own_ref[0, :, at], grad_ref[:rows]) + tn(
            sib_ref[0, :, at], grad_ref[rows:]
        )
        for h in range(heads):
            cut = slice(h * HD, (h + 1) * HD)
            ref[0, :, wide + h * tall : wide + (h + 1) * tall] = tn(
                ctx_ref[:rows, cut], own_ref[1, :, at]
            ) + tn(ctx_ref[rows:, cut], sib_ref[1, :, at])

    piece(0, 1 + 2 * step, ax_ref)
    piece(1, 2 + step, by_ref)
    piece(0, 2 * step, ak_ref)
    piece(1, step, bk_ref)


def weight_grads(meta, own, sib, ctx, grad):
    _, rows, width = own.shape
    tall = width // 8
    columns = grad.shape[1] + ctx.shape[1] // HD * tall
    out = jax.ShapeDtypeStruct((2, tall, columns), jnp.float32)
    return pl.pallas_call(
        grads_kernel,
        grid_spec=pltpu.PrefetchScalarGridSpec(
            num_scalar_prefetch=1,
            grid=(2,),
            in_specs=[whole()] * 4,
            out_specs=[pl.BlockSpec((1, tall, columns), lambda i, m: (i, 0, 0))] * 4,
        ),
        out_shape=[out] * 4,
        compiler_params=params(),
        cost_estimate=cost(4 * rows * width * columns, 16 * width * columns),
        name="weight_grads",
    )(meta, own, sib, ctx, grad)


def place_kernel(pieces, groups, meta, *refs):
    own, sib, outs = refs[:groups], refs[groups : 2 * groups], refs[-4:]
    step = pl.program_id(0)
    first = meta[1] == 0
    wq, wk, wv, wo = outs
    tall = wq.shape[0]
    q, k = wq.shape[1] // 2, wk.shape[1] // 2
    heads = wo.shape[0] // (2 * HD)

    def pick(group, route, j):
        if j < 3:
            return group[j][route]
        return group[route][...]

    for route in range(2):
        for place, j in enumerate(pieces):

            @pl.when(step == route * len(pieces) + place)
            def _():
                mine, other = pick(own, route, j), pick(sib, route, j)
                for side, block in enumerate(
                    (jnp.where(first, mine, other), jnp.where(first, other, mine))
                ):
                    wq[:, side * q : (side + 1) * q] = block[:, :q]
                    wk[:, side * k : (side + 1) * k] = block[:, q : q + k]
                    wv[:, side * k : (side + 1) * k] = block[:, q + k : q + 2 * k]
                    for h in range(heads):
                        row = (side * heads + h) * HD
                        cut = q + 2 * k + h * tall
                        wo[row : row + HD] = block[:, cut : cut + tall]


def place_grads(meta, own, sib, shapes, pieces, into=()):
    tall = own[0].shape[-2]
    size = len(pieces)

    def spot(i, m):
        return (i // size) * 4 + (m[0] ^ (i % size + pieces[0]))

    rows = lambda s: pl.BlockSpec((tall, s[1]), lambda i, m: (spot(i, m), 0))
    specs = [rows(s) for s in shapes[:3]]
    specs.append(pl.BlockSpec((shapes[3][0], tall), lambda i, m: (0, spot(i, m))))
    inputs = 2 * len(own)
    return pl.pallas_call(
        functools.partial(place_kernel, tuple(pieces), len(own)),
        grid_spec=pltpu.PrefetchScalarGridSpec(
            num_scalar_prefetch=1,
            grid=(2 * size,),
            in_specs=[whole()] * inputs + [pl.BlockSpec(memory_space=pl.ANY)] * len(into),
            out_specs=specs,
        ),
        out_shape=[jax.ShapeDtypeStruct(s, jnp.float32) for s in shapes],
        input_output_aliases={1 + inputs + n: n for n in range(len(into))},
        compiler_params=params(),
        cost_estimate=cost(0, size * 2 * sum(s[0] * s[1] for s in shapes)),
        name="place_grads",
    )(meta, *own, *sib, *into)


def context_part(meta, ref, j, quarter):
    side = ref.shape[1] // 2
    at = (meta[0] ^ j) * quarter
    head = ((at // side) ^ meta[1]) * side + at % side
    return ref[:, pl.ds(pl.multiple_of(head, quarter), quarter)]


def near_kernel(meta, tok_ref, *refs):
    contexts, own, sib, out_ref = refs[:3], refs[3:6], refs[6:9], refs[9]
    step = pl.program_id(0)
    quarter = own[0].shape[1]

    def run(group):
        for k, ref in enumerate(contexts):
            total = nn(context_part(meta, ref, 0, quarter), group[0][k])
            for j in range(1, 3):
                total += nn(context_part(meta, ref, j, quarter), group[j][k])
            if k == 0:
                out_ref[...] = tok_ref[...].astype(jnp.float32) + total
            else:
                out_ref[...] += total

    @pl.when(step == 0)
    def _():
        run(own)

    @pl.when(step == 1)
    def _():
        run(sib)


def output_near(meta, flat, contexts, own, sib):
    count = flat.shape[0]
    half = own[0].shape[2]
    wide = contexts[0].shape[1]
    return pl.pallas_call(
        near_kernel,
        grid_spec=pltpu.PrefetchScalarGridSpec(
            num_scalar_prefetch=1,
            grid=(2,),
            in_specs=[pl.BlockSpec((count, half), lambda i, m: (0, 2 * m[2] + (m[1] ^ i)))]
            + [whole()] * 9,
            out_specs=pl.BlockSpec((count, half), lambda i, m: (0, m[1] ^ i)),
        ),
        out_shape=jax.ShapeDtypeStruct((count, 2 * half), jnp.float32),
        compiler_params=params(),
        cost_estimate=cost(12 * count * wide * half, 32 * wide * half),
        name="output_near",
    )(meta, flat, *contexts, *own[:3], *sib[:3])


def far_kernel(meta, sum_ref, c0, c1, c2, c3, *refs):
    own, sib, out_ref = refs[:5], refs[5:10], refs[10]
    step = pl.program_id(0)
    quarter = own[0].shape[1]

    def run(group):
        total = sum_ref[...]
        for k, ref in enumerate((c0, c1, c2, c3)):
            total += nn(context_part(meta, ref, 3, quarter), group[3 + k // 2][k % 2])
        for j in range(3):
            total += nn(context_part(meta, c3, j, quarter), group[j][0])
        out_ref[...] = total.astype(jnp.bfloat16)

    @pl.when(step == 0)
    def _():
        run(own)

    @pl.when(step == 1)
    def _():
        run(sib)


def output_far(meta, near, contexts, own, sib):
    count, columns = near.shape
    half = columns // 2
    quarter = own[0].shape[1]
    slots = [pl.BlockSpec((1, quarter, half), lambda i, m: (3, 0, 0))] * 3 + [whole()] * 2
    return pl.pallas_call(
        far_kernel,
        grid_spec=pltpu.PrefetchScalarGridSpec(
            num_scalar_prefetch=1,
            grid=(2,),
            in_specs=[pl.BlockSpec((count, half), lambda i, m: (0, m[1] ^ i))]
            + [whole()] * 4
            + slots * 2,
            out_specs=pl.BlockSpec((count, half), lambda i, m: (0, m[1] ^ i)),
        ),
        out_shape=jax.ShapeDtypeStruct((count, columns), jnp.bfloat16),
        compiler_params=params(),
        cost_estimate=cost(4 * count * 7 * quarter * half, 8 * count * columns),
        name="output_far",
    )(meta, near, *contexts, *own, *sib)


def plane_body(
    prefix_tokens,
    prefix_len,
    causal_start,
    span_sample,
    bb_wq,
    bb_wk,
    bb_wv,
    bb_wo,
    action_tokens,
    ex_wq,
    ex_wk,
    ex_wv,
    ex_wo,
    action_cot,
):
    samples, positions, width = prefix_tokens.shape
    factor = 1.0 / math.sqrt(HD)
    count = samples * positions
    flat = prefix_tokens.reshape(count, width)
    device = lax.axis_index("dp")
    chip, core = device // 2, device % 2
    plane = lax.axis_index("tensor")

    def across(mask):
        return lambda x: lax.ppermute(x, "dp", [(i, i ^ mask) for i in range(8)])

    swap, over_x, over_y = across(1), across(2), across(4)

    def after(x, *others):
        return lax.optimization_barrier((x, *others))[0]

    local = jnp.concatenate([prefix_len, causal_start, span_sample])
    remote = swap(local)
    meta = jnp.concatenate(
        [
            jnp.stack([chip, core, plane, 0]).astype(jnp.int32),
            local[:2],
            remote[:2],
            local[2:4],
            remote[2:4],
            local[4:],
            remote[4:] + samples,
        ]
    )
    chip_meta = jnp.stack([chip, core, plane, 0]).astype(jnp.int32)

    def halves(weight):
        size = weight.shape[1] // 2
        mine = lax.dynamic_slice_in_dim(weight, core * size, size, 1)
        other = lax.dynamic_slice_in_dim(weight, (1 - core) * size, size, 1)
        return mine, other

    k_mine, k_other = halves(bb_wk)
    v_mine, v_other = halves(bb_wv)
    q_mine, q_other = halves(bb_wq)
    kv_got = swap(jnp.concatenate([k_other, v_other], axis=1))
    kv_shard = jnp.concatenate([jnp.concatenate([k_mine, v_mine], axis=1), kv_got])
    kv_x, kv_y = over_x(kv_shard), over_y(kv_shard)

    q_got = swap(after(q_other, kv_shard))
    spans = action_tokens.shape[0]
    pad = ((0, 0), (0, PAD - STEPS), (0, 0))
    pair = jnp.stack([jnp.pad(action_tokens, pad), jnp.pad(action_cot, pad)])
    pair = pair.reshape(2, spans * PAD, action_tokens.shape[2])
    pair_sib = swap(after(pair, kv_shard))
    normed = normalise(chip_meta, after(flat, q_got, pair_sib), 4)
    normed_sib = swap(after(normed, kv_x, kv_y))
    half = kv_x.shape[0] // 2
    low, high = kv_y[:half], kv_x[half:]
    kv_dx, kv_dy = over_x(low), over_y(high)
    proj, dctx = expert_project(
        chip_meta, after(pair, low, high), pair_sib, ex_wq, ex_wk, ex_wv, ex_wo
    )
    q_shard = after(jnp.concatenate([q_mine, q_got]), kv_dx, kv_dy, normed_sib, proj)
    q_x, q_y = over_x(q_shard), over_y(q_shard)

    quarter = bb_wo.shape[0] // 4
    wo_rows = after(bb_wo, q_shard)
    by_chip = [
        lax.dynamic_slice_in_dim(wo_rows, (chip ^ m) * quarter, quarter, 0) for m in range(4)
    ]
    wo_a = [by_chip[0], over_x(by_chip[1]), over_y(by_chip[2]), across(6)(by_chip[3])]

    kv = project_kv(normed, normed_sib, (kv_shard, kv_x, kv_y, kv_dx, kv_dy))
    ectx, egrad = expert_attend(meta, proj, dctx, kv, factor)
    low, high = after(q_y, ectx, *wo_a)[:half], after(q_x, ectx, *wo_a)[half:]
    q_dx, q_dy = over_x(low), over_y(high)
    wo_a = jnp.stack(wo_a)
    wo_b = []
    for s in range(4):
        piece = lax.dynamic_index_in_dim(
            wo_a, chip ^ lax.rem(plane + s, 4), 0, keepdims=False
        )
        perm = [(i, (i + s) % 4) for i in range(4)]
        wo_b.append(lax.ppermute(piece, "tensor", perm) if s else piece)

    ax, ak, by, bk = weight_grads(chip_meta, pair, pair_sib, after(ectx, low, high), egrad)
    a_got, b_got = over_x(ax), over_y(by)
    ctx = attend(
        meta, normed, normed_sib, (q_shard, q_x, q_y, q_dx, q_dy), after(kv, ax), positions, factor
    )
    ctx_own, ctx_other = ctx
    wo_b = [after(x, ctx_own) for x in wo_b]
    a_got, b_got = after(a_got, ctx_own), after(b_got, ctx_own)
    ctx_got = swap(after(ctx_other, a_got, b_got, *wo_b))
    ctx_rows = jnp.concatenate([ctx_own, ctx_got], axis=1)
    turn = lambda x: lax.ppermute(x, "tensor", [(i, (i + 1) % 4) for i in range(4)])
    ctx_1 = turn(ctx_rows)
    a_sum, b_sum = ak + a_got, bk + b_got
    a_rest, b_rest = over_y(a_sum[1]), over_x(b_sum[1])
    mine = jnp.stack([a_sum[0] + a_rest, b_sum[0] + b_rest])
    wo = after(jnp.stack([after(x, ctx_got) for x in wo_b]), a_rest, b_rest)
    wo_x, wo_y = over_x(wo), over_y(wo)
    sent = after(mine, wo_x, wo_y)
    from_x, from_y = over_x(sent), over_y(sent)
    ctx_2 = turn(ctx_1)
    wo_sib = [swap(after(wo, wo_x)), swap(wo_x), swap(wo_y)]
    wo_dx = over_x(after(wo_y, from_x, from_y)[:2])
    wo_dy = over_y(after(wo_x, from_x, from_y)[2:])
    ctx_3 = turn(ctx_2)
    near = output_near(chip_meta, flat, (ctx_rows, ctx_1, ctx_2), (wo, wo_x, wo_y), wo_sib)
    far_x = over_x(after(from_y, wo_dx, wo_dy)[0])
    far_y = over_y(after(from_x, wo_dx, wo_dy)[1])
    near_grads = (mine, from_x, from_y)
    near_sib = tuple(swap(x) for x in near_grads)
    shapes = (ex_wq.shape, ex_wk.shape, ex_wv.shape, ex_wo.shape)
    grads = place_grads(chip_meta, near_grads, near_sib, shapes, range(3))
    wo_own = (wo, wo_x, wo_y, wo_dx, wo_dy)
    wo_sib += [swap(wo_dx), swap(wo_dy)]
    far = (far_x, far_y)
    grads = place_grads(chip_meta, far, [swap(x) for x in far], shapes, range(3, 4), grads)
    out = output_far(chip_meta, near, (ctx_rows, ctx_1, ctx_2, ctx_3), wo_own, wo_sib)
    return (out.reshape(samples, positions, -1), *grads)


def fits_plane(mesh):
    return mesh.shape["dp"] == 8 and mesh.shape["tensor"] == 4


def solution(mesh):
    in_specs = (
        P("dp", None, None),
        P("dp"),
        P("dp"),
        P("dp"),
        P("dp", "tensor"),
        P("dp", "tensor"),
        P("dp", "tensor"),
        P("tensor", "dp"),
        P("dp", None, None),
        P(None, "tensor"),
        P(None, "tensor"),
        P(None, "tensor"),
        P("tensor", None),
        P("dp", None, None),
    )
    out_specs = (
        P("dp", None, "tensor"),
        P(None, "tensor"),
        P(None, "tensor"),
        P(None, "tensor"),
        P("tensor", None),
    )
    body = plane_body if fits_plane(mesh) else general_body
    return jax.shard_map(body, mesh=mesh, in_specs=in_specs, out_specs=out_specs, check_vma=False)
```

```python
import functools
import math

import jax
import jax.numpy as jnp
from jax import lax
from jax.experimental import pallas as pl
from jax.experimental.pallas import tpu as pltpu
from jax.sharding import PartitionSpec as P

HD = 128
STEPS = 50


def general_body(
    prefix_tokens,
    prefix_len,
    causal_start,
    span_sample,
    bb_wq,
    bb_wk,
    bb_wv,
    bb_wo,
    action_tokens,
    ex_wq,
    ex_wk,
    ex_wv,
    ex_wo,
    action_cot,
):
    samples, positions, width = prefix_tokens.shape
    factor = 1.0 / math.sqrt(HD)
    kv_local = bb_wk.shape[1] // HD
    group = bb_wq.shape[1] // bb_wk.shape[1]
    egroup = ex_wq.shape[1] // ex_wk.shape[1]
    count = samples * positions
    flat = prefix_tokens.reshape(count, width)
    widened = flat.astype(jnp.float32)
    normed = (
        widened * lax.rsqrt(jnp.mean(widened * widened, axis=-1, keepdims=True) + 1e-06)
    ).astype(jnp.bfloat16)
    pieces = (
        lax.all_gather(bb_wq, "dp", axis=0, tiled=True),
        lax.all_gather(bb_wk, "dp", axis=0, tiled=True),
        lax.all_gather(bb_wv, "dp", axis=0, tiled=True),
    )
    query_sum, key_sum, value_sum = tuple(
        (jnp.dot(normed, piece, preferred_element_type=jnp.float32) for piece in pieces)
    )
    query = query_sum.astype(jnp.bfloat16).reshape(samples, positions, kv_local, group, HD)
    keys = key_sum.astype(jnp.bfloat16).reshape(samples, positions, kv_local, HD)
    values = value_sum.astype(jnp.bfloat16).reshape(samples, positions, kv_local, HD)
    scores = (
        jnp.einsum("sigeh,sjgh->sgeij", query, keys, preferred_element_type=jnp.float32) * factor
    )
    places = jnp.arange(positions, dtype=jnp.int32)
    length_view = prefix_len[:, None, None, None, None]
    start_view = causal_start[:, None, None, None, None]
    visible = (places[None, None, None, None, :] < length_view) & (
        (places[None, None, None, None, :] < start_view)
        | (places[None, None, None, None, :] <= places[None, None, None, :, None])
    )
    scores = jnp.where(visible, scores, -1e30)
    top = jnp.max(scores, axis=-1, keepdims=True)
    weights = jnp.where(visible, jnp.exp(scores - top), 0.0)
    weights = (weights / jnp.sum(weights, axis=-1, keepdims=True)).astype(jnp.bfloat16)
    context = (
        jnp.einsum("sgeij,sjgh->sigeh", weights, values, preferred_element_type=jnp.float32)
        .astype(jnp.bfloat16)
        .reshape(count, bb_wq.shape[1])
    )
    partial_out = jnp.dot(
        context, lax.all_gather(bb_wo, "dp", axis=1, tiled=True), preferred_element_type=jnp.float32
    )
    summed = lax.psum_scatter(partial_out, "tensor", scatter_dimension=1, tiled=True)
    share = summed.shape[1]
    residual = lax.dynamic_slice_in_dim(widened, lax.axis_index("tensor") * share, share, 1)
    prefix_out = (residual + summed).astype(jnp.bfloat16).reshape(samples, positions, share)
    spans = action_tokens.shape[0]
    rows = spans * STEPS
    action_flat = action_tokens.reshape(rows, action_tokens.shape[2])
    cot_flat = action_cot.reshape(rows, action_cot.shape[2])
    pre_keys = jnp.take(keys, span_sample, axis=0)
    pre_values = jnp.take(values, span_sample, axis=0)
    span_length = jnp.take(prefix_len, span_sample, axis=0)
    equery = (
        jnp.dot(action_flat, ex_wq, preferred_element_type=jnp.float32)
        .astype(jnp.bfloat16)
        .reshape(spans, STEPS, kv_local, egroup, HD)
    )
    own_keys = (
        jnp.dot(action_flat, ex_wk, preferred_element_type=jnp.float32)
        .astype(jnp.bfloat16)
        .reshape(spans, STEPS, kv_local, HD)
    )
    own_values = (
        jnp.dot(action_flat, ex_wv, preferred_element_type=jnp.float32)
        .astype(jnp.bfloat16)
        .reshape(spans, STEPS, kv_local, HD)
    )
    valid = (places[None, :] < span_length[:, None])[:, None, None, None, :]
    score_pre = (
        jnp.einsum("ctgeh,cpgh->cgetp", equery, pre_keys, preferred_element_type=jnp.float32)
        * factor
    )
    score_pre = jnp.where(valid, score_pre, -1e30)
    score_own = (
        jnp.einsum("ctgeh,cugh->cgetu", equery, own_keys, preferred_element_type=jnp.float32)
        * factor
    )
    peak = jnp.maximum(jnp.max(score_pre, axis=-1), jnp.max(score_own, axis=-1))[..., None]
    exp_pre = jnp.where(valid, jnp.exp(score_pre - peak), 0.0)
    exp_own = jnp.exp(score_own - peak)
    total = jnp.sum(exp_pre, axis=-1, keepdims=True) + jnp.sum(exp_own, axis=-1, keepdims=True)
    prob_pre = exp_pre / total
    prob_own = exp_own / total
    half_pre = prob_pre.astype(jnp.bfloat16)
    half_own = prob_own.astype(jnp.bfloat16)
    econtext = (
        jnp.einsum("cgetp,cpgh->ctgeh", half_pre, pre_values, preferred_element_type=jnp.float32)
        + jnp.einsum("cgetu,cugh->ctgeh", half_own, own_values, preferred_element_type=jnp.float32)
    ).astype(jnp.bfloat16)
    econtext_flat = econtext.reshape(rows, ex_wq.shape[1])
    grad_out_local = jnp.einsum(
        "ti,tj->ij", econtext_flat, cot_flat, preferred_element_type=jnp.float32
    )
    dcontext = (
        jnp.einsum("tj,ij->ti", cot_flat, ex_wo, preferred_element_type=jnp.float32)
        .astype(jnp.bfloat16)
        .reshape(spans, STEPS, kv_local, egroup, HD)
    )
    dprob_pre = jnp.einsum(
        "ctgeh,cpgh->cgetp", dcontext, pre_values, preferred_element_type=jnp.float32
    )
    dprob_own = jnp.einsum(
        "ctgeh,cugh->cgetu", dcontext, own_values, preferred_element_type=jnp.float32
    )
    delta = (jnp.sum(prob_pre * dprob_pre, axis=-1) + jnp.sum(prob_own * dprob_own, axis=-1))[
        ..., None
    ]
    dscore_pre = (prob_pre * (dprob_pre - delta) * factor).astype(jnp.bfloat16)
    dscore_own = (prob_own * (dprob_own - delta) * factor).astype(jnp.bfloat16)
    dquery = (
        jnp.einsum("cgetp,cpgh->ctgeh", dscore_pre, pre_keys, preferred_element_type=jnp.float32)
        + jnp.einsum("cgetu,cugh->ctgeh", dscore_own, own_keys, preferred_element_type=jnp.float32)
    ).astype(jnp.bfloat16)
    dkeys = jnp.einsum(
        "cgetu,ctgeh->cugh", dscore_own, equery, preferred_element_type=jnp.float32
    ).astype(jnp.bfloat16)
    dvalues = jnp.einsum(
        "cgetu,ctgeh->cugh", half_own, dcontext, preferred_element_type=jnp.float32
    ).astype(jnp.bfloat16)
    grad_query_local = jnp.einsum(
        "ti,tj->ij",
        action_flat,
        dquery.reshape(rows, ex_wq.shape[1]),
        preferred_element_type=jnp.float32,
    )
    grad_key_local = jnp.einsum(
        "ti,tj->ij",
        action_flat,
        dkeys.reshape(rows, ex_wk.shape[1]),
        preferred_element_type=jnp.float32,
    )
    grad_value_local = jnp.einsum(
        "ti,tj->ij",
        action_flat,
        dvalues.reshape(rows, ex_wv.shape[1]),
        preferred_element_type=jnp.float32,
    )
    grad_wq, grad_wk, grad_wv, grad_wo = lax.psum(
        (grad_query_local, grad_key_local, grad_value_local, grad_out_local), "dp"
    )
    return (prefix_out, grad_wq, grad_wk, grad_wv, grad_wo)


NEG = -1e30
PAD = 64
HIGH = 56 * 1024 * 1024
LOW = 32 * 1024 * 1024


def params(limit=HIGH):
    return pltpu.CompilerParams(vmem_limit_bytes=limit)


def cost(flops, moved):
    return pl.CostEstimate(flops=int(flops), bytes_accessed=int(moved), transcendentals=0)


def whole():
    return pl.BlockSpec(memory_space=pltpu.VMEM)


def nt(a, b):
    return lax.dot_general(a, b, (((1,), (1,)), ((), ())), preferred_element_type=jnp.float32)


def tn(a, b):
    return lax.dot_general(a, b, (((0,), (0,)), ((), ())), preferred_element_type=jnp.float32)


def nn(a, b):
    return jnp.dot(a, b, preferred_element_type=jnp.float32)


def norm_kernel(meta, x_ref, out_ref):
    chip, core = meta[0], meta[1]
    parts, rows, wide = out_ref.shape
    half = wide // 2
    x = x_ref[...].astype(jnp.float32)
    scale = lax.rsqrt(jnp.mean(x * x, axis=-1, keepdims=True) + 1e-06)
    for j in range(parts):
        for side in range(2):
            at = pl.multiple_of(((chip ^ j) * 2 + (core ^ side)) * half, half)
            piece = x_ref[:, pl.ds(at, half)].astype(jnp.float32)
            out_ref[j, :, side * half : (side + 1) * half] = (piece * scale).astype(jnp.bfloat16)


def normalise(meta, flat, parts):
    count, width = flat.shape
    block = 128
    return pl.pallas_call(
        norm_kernel,
        grid_spec=pltpu.PrefetchScalarGridSpec(
            num_scalar_prefetch=1,
            grid=(count // block,),
            in_specs=[pl.BlockSpec((block, width), lambda i, m: (i, 0))],
            out_specs=pl.BlockSpec((parts, block, width // parts), lambda i, m: (0, i, 0)),
        ),
        out_shape=jax.ShapeDtypeStruct((parts, count, width // parts), jnp.bfloat16),
        compiler_params=params(),
        cost_estimate=cost(4 * count * width, 4 * count * width),
        name="normalise",
    )(meta, flat)


def product(ref, weights, swapped):
    w0, w1, w2, wx, wy = weights
    half = wx.shape[0]
    first, second = slice(0, half), slice(half, 2 * half)
    if not swapped:
        total = nn(ref[0], w0[...]) + nn(ref[1], w1[...]) + nn(ref[2], w2[...])
        return total + nn(ref[3, :, first], wx[...]) + nn(ref[3, :, second], wy[...])
    total = nn(ref[3, :, second], wx[...]) + nn(ref[3, :, first], wy[...])
    for j, weight in enumerate((w0, w1, w2)):
        total += nn(ref[j, :, second], weight[first]) + nn(ref[j, :, first], weight[second])
    return total


def kv_kernel(own_ref, sib_ref, w0, w1, w2, wx, wy, out_ref):
    step = pl.program_id(0)
    half = pl.num_programs(0) // 2
    weights = (w0, w1, w2, wx, wy)

    @pl.when(step < half)
    def _():
        out_ref[...] = product(own_ref, weights, False).astype(jnp.bfloat16)

    @pl.when(step >= half)
    def _():
        out_ref[...] = product(sib_ref, weights, True).astype(jnp.bfloat16)


def pair_specs(parts, block, wide, steps, sib_first=False):
    first = pl.BlockSpec(
        (parts, block, wide), lambda i, *m: (0, jnp.minimum(i, steps // 2 - 1), 0)
    )
    then = pl.BlockSpec((parts, block, wide), lambda i, *m: (0, jnp.maximum(i - steps // 2, 0), 0))
    return [then, first] if sib_first else [first, then]


def project_kv(own, sib, weights):
    parts, count, wide = own.shape
    columns = weights[0].shape[1]
    block = 256
    steps = 2 * count // block
    return pl.pallas_call(
        kv_kernel,
        grid=(steps,),
        in_specs=pair_specs(parts, block, wide, steps) + [whole()] * 5,
        out_specs=pl.BlockSpec((block, columns), lambda i: (i, 0)),
        out_shape=jax.ShapeDtypeStruct((2 * count, columns), jnp.bfloat16),
        compiler_params=params(),
        cost_estimate=cost(4 * count * parts * wide * columns, 4 * count * parts * wide),
        name="project_kv",
    )(own, sib, *weights)


def attend_kernel(factor, meta, own_ref, sib_ref, w0, w1, w2, wx, wy, kv_ref, own_out, sib_out, query, context):
    step = pl.program_id(0)
    half = pl.num_programs(0) // 2
    weights = (w0, w1, w2, wx, wy)

    @pl.when(step >= half)
    def _():
        query[...] = product(own_ref, weights, False).astype(jnp.bfloat16)

    @pl.when(step < half)
    def _():
        query[...] = product(sib_ref, weights, True).astype(jnp.bfloat16)

    sample = lax.rem(step + half, 2 * half)
    length = meta[4 + sample]
    start = meta[8 + sample]
    positions = context.shape[0]
    keys = kv_ref[:, :HD]
    values = kv_ref[:, HD:]
    row = lax.broadcasted_iota(jnp.int32, (positions, positions), 0)
    column = lax.broadcasted_iota(jnp.int32, (positions, positions), 1)
    visible = (column < length) & ((column < start) | (column <= row))
    for head in range(context.shape[1] // HD):
        at = slice(head * HD, (head + 1) * HD)
        scores = jnp.where(visible, nt(query[:, at], keys) * factor, NEG)
        top = jnp.max(scores, axis=-1, keepdims=True)
        weight = jnp.where(visible, jnp.exp(scores - top), 0.0)
        weight = (weight / jnp.sum(weight, axis=-1, keepdims=True)).astype(jnp.bfloat16)
        context[:, at] = nn(weight, values).astype(jnp.bfloat16)

    @pl.when(step >= half)
    def _():
        own_out[...] = context[...]

    @pl.when(step < half)
    def _():
        sib_out[...] = context[...]


def attend(meta, own, sib, weights, kv, positions, factor):
    parts, count, wide = own.shape
    columns = weights[0].shape[1]
    steps = 2 * count // positions
    half = steps // 2
    out = jax.ShapeDtypeStruct((count, columns), jnp.bfloat16)
    return pl.pallas_call(
        functools.partial(attend_kernel, factor),
        grid_spec=pltpu.PrefetchScalarGridSpec(
            num_scalar_prefetch=1,
            grid=(steps,),
            in_specs=pair_specs(parts, positions, wide, steps, True)
            + [whole()] * 5
            + [pl.BlockSpec((positions, 2 * HD), lambda i, m: ((i + half) % steps, 0))],
            out_specs=[
                pl.BlockSpec((positions, columns), lambda i, m: (jnp.maximum(i - half, 0), 0)),
                pl.BlockSpec((positions, columns), lambda i, m: (jnp.minimum(i, half - 1), 0)),
            ],
            scratch_shapes=[pltpu.VMEM((positions, columns), jnp.bfloat16)] * 2,
        ),
        out_shape=[out, out],
        compiler_params=params(),
        cost_estimate=cost(8 * count * parts * wide * columns, 4 * count * parts * wide),
        name="attend",
    )(meta, own, sib, *weights, kv)


def expert_project_kernel(meta, own_ref, sib_ref, wq, wk, wv, wo, out_ref, cot_ref):
    step = pl.program_id(0)
    half = pl.num_programs(0) // 2

    def run(ref):
        action = ref[0]
        q, k = wq.shape[1], wk.shape[1]
        out_ref[:, :q] = nn(action, wq[...]).astype(jnp.bfloat16)
        out_ref[:, q : q + k] = nn(action, wk[...]).astype(jnp.bfloat16)
        out_ref[:, q + k :] = nn(action, wv[...]).astype(jnp.bfloat16)
        cot_ref[...] = nt(ref[1], wo[...]).astype(jnp.bfloat16)

    @pl.when(step < half)
    def _():
        run(own_ref)

    @pl.when(step >= half)
    def _():
        run(sib_ref)


def expert_project(meta, own, sib, wq, wk, wv, wo):
    _, rows, width = own.shape
    block = 256
    steps = 2 * rows // block
    q, k = wq.shape[1] // 2, wk.shape[1] // 2
    return pl.pallas_call(
        expert_project_kernel,
        grid_spec=pltpu.PrefetchScalarGridSpec(
            num_scalar_prefetch=1,
            grid=(steps,),
            in_specs=pair_specs(2, block, width, steps)
            + [
                pl.BlockSpec((width, q), lambda i, m: (0, m[1])),
                pl.BlockSpec((width, k), lambda i, m: (0, m[1])),
                pl.BlockSpec((width, k), lambda i, m: (0, m[1])),
                pl.BlockSpec((q, width), lambda i, m: (m[1], 0)),
            ],
            out_specs=[
                pl.BlockSpec((block, q + 2 * k), lambda i, m: (i, 0)),
                pl.BlockSpec((block, q), lambda i, m: (i, 0)),
            ],
        ),
        out_shape=[
            jax.ShapeDtypeStruct((2 * rows, q + 2 * k), jnp.bfloat16),
            jax.ShapeDtypeStruct((2 * rows, q), jnp.bfloat16),
        ],
        compiler_params=params(),
        cost_estimate=cost(4 * rows * width * (2 * q + 2 * k), 8 * rows * width),
        name="expert_project",
    )(meta, own, sib, wq, wk, wv, wo)


def expert_kernel(factor, spans, meta, proj_ref, dctx_ref, kv_ref, ctx_ref, grad_ref):
    step = pl.program_id(0)
    positions = meta.shape[0] and 256
    width = dctx_ref.shape[1]
    heads = width // HD
    rows = heads * PAD
    own_column = lax.broadcasted_iota(jnp.int32, (rows, PAD), 1)
    pre_column = lax.broadcasted_iota(jnp.int32, (rows, positions), 1)
    for s in range(spans):
        sample = meta[12 + step * spans + s]
        valid = pre_column < meta[4 + sample]
        own_valid = own_column < STEPS
        at = slice(s * PAD, (s + 1) * PAD)
        base = pl.multiple_of(sample * positions, positions)
        pre_keys = kv_ref[pl.ds(base, positions), :HD]
        pre_values = kv_ref[pl.ds(base, positions), HD:]
        stack = lambda ref: jnp.concatenate(
            [ref[at, h * HD : (h + 1) * HD] for h in range(heads)], axis=0
        )
        query = stack(proj_ref)
        cot = stack(dctx_ref)
        own_keys = proj_ref[at, width : width + HD]
        own_values = proj_ref[at, width + HD :]
        score_pre = jnp.where(valid, nt(query, pre_keys) * factor, NEG)
        score_own = jnp.where(own_valid, nt(query, own_keys) * factor, NEG)
        peak = jnp.maximum(
            jnp.max(score_pre, axis=-1, keepdims=True), jnp.max(score_own, axis=-1, keepdims=True)
        )
        exp_pre = jnp.where(valid, jnp.exp(score_pre - peak), 0.0)
        exp_own = jnp.where(own_valid, jnp.exp(score_own - peak), 0.0)
        total = jnp.sum(exp_pre, axis=-1, keepdims=True) + jnp.sum(exp_own, axis=-1, keepdims=True)
        prob_pre = exp_pre / total
        prob_own = exp_own / total
        half_pre = prob_pre.astype(jnp.bfloat16)
        half_own = prob_own.astype(jnp.bfloat16)
        context = (nn(half_pre, pre_values) + nn(half_own, own_values)).astype(jnp.bfloat16)
        dprob_pre = nt(cot, pre_values)
        dprob_own = nt(cot, own_values)
        delta = jnp.sum(prob_pre * dprob_pre, axis=-1, keepdims=True) + jnp.sum(
            prob_own * dprob_own, axis=-1, keepdims=True
        )
        dscore_pre = (prob_pre * (dprob_pre - delta) * factor).astype(jnp.bfloat16)
        dscore_own = (prob_own * (dprob_own - delta) * factor).astype(jnp.bfloat16)
        dquery = (nn(dscore_pre, pre_keys) + nn(dscore_own, own_keys)).astype(jnp.bfloat16)
        for h in range(heads):
            part = slice(h * PAD, (h + 1) * PAD)
            ctx_ref[at, h * HD : (h + 1) * HD] = context[part]
            grad_ref[at, h * HD : (h + 1) * HD] = dquery[part]
        grad_ref[at, width : width + HD] = tn(dscore_own, query).astype(jnp.bfloat16)
        grad_ref[at, width + HD :] = tn(half_own, cot).astype(jnp.bfloat16)


def expert_attend(meta, proj, dctx, kv, factor):
    rows, columns = proj.shape
    width = dctx.shape[1]
    spans = 4
    steps = rows // (PAD * spans)
    block = PAD * spans
    return pl.pallas_call(
        functools.partial(expert_kernel, factor, spans),
        grid_spec=pltpu.PrefetchScalarGridSpec(
            num_scalar_prefetch=1,
            grid=(steps,),
            in_specs=[
                pl.BlockSpec((block, columns), lambda i, m: (i, 0)),
                pl.BlockSpec((block, width), lambda i, m: (i, 0)),
                whole(),
            ],
            out_specs=[
                pl.BlockSpec((block, width), lambda i, m: (i, 0)),
                pl.BlockSpec((block, columns), lambda i, m: (i, 0)),
            ],
        ),
        out_shape=[
            jax.ShapeDtypeStruct((rows, width), jnp.bfloat16),
            jax.ShapeDtypeStruct((rows, columns), jnp.bfloat16),
        ],
        compiler_params=params(LOW),
        cost_estimate=cost(40 * rows * 320 * width, 8 * rows * columns),
        name="expert_attend",
    )(meta, proj, dctx, kv)


def grads_kernel(meta, own_ref, sib_ref, ctx_ref, grad_ref, ax_ref, ak_ref, by_ref, bk_ref):
    chip = meta[0]
    step = pl.program_id(0)
    rows = own_ref.shape[1]
    tall = ax_ref.shape[1]
    wide = grad_ref.shape[1]
    heads = ctx_ref.shape[1] // HD

    def piece(route, j, ref):
        at = pl.ds(pl.multiple_of((route * 4 + (chip ^ j)) * tall, tall), tall)
        ref[0, :, :wide] = tn(own_ref[0, :, at], grad_ref[:rows]) + tn(
            sib_ref[0, :, at], grad_ref[rows:]
        )
        for h in range(heads):
            cut = slice(h * HD, (h + 1) * HD)
            ref[0, :, wide + h * tall : wide + (h + 1) * tall] = tn(
                ctx_ref[:rows, cut], own_ref[1, :, at]
            ) + tn(ctx_ref[rows:, cut], sib_ref[1, :, at])

    piece(0, 1 + 2 * step, ax_ref)
    piece(1, 2 + step, by_ref)
    piece(0, 2 * step, ak_ref)
    piece(1, step, bk_ref)


def weight_grads(meta, own, sib, ctx, grad):
    _, rows, width = own.shape
    tall = width // 8
    columns = grad.shape[1] + ctx.shape[1] // HD * tall
    out = jax.ShapeDtypeStruct((2, tall, columns), jnp.float32)
    return pl.pallas_call(
        grads_kernel,
        grid_spec=pltpu.PrefetchScalarGridSpec(
            num_scalar_prefetch=1,
            grid=(2,),
            in_specs=[whole()] * 4,
            out_specs=[pl.BlockSpec((1, tall, columns), lambda i, m: (i, 0, 0))] * 4,
        ),
        out_shape=[out] * 4,
        compiler_params=params(LOW),
        cost_estimate=cost(4 * rows * width * columns, 16 * width * columns),
        name="weight_grads",
    )(meta, own, sib, ctx, grad)


def place_kernel(pieces, groups, meta, *refs):
    own, sib, outs = refs[:groups], refs[groups : 2 * groups], refs[-4:]
    step = pl.program_id(0)
    first = meta[1] == 0
    wq, wk, wv, wo = outs
    tall = wq.shape[0]
    q, k = wq.shape[1] // 2, wk.shape[1] // 2
    heads = wo.shape[0] // (2 * HD)

    def pick(group, route, j):
        if j < 3:
            return group[j][route]
        return group[route][...]

    for route in range(2):
        for place, j in enumerate(pieces):

            @pl.when(step == route * len(pieces) + place)
            def _():
                mine, other = pick(own, route, j), pick(sib, route, j)
                for side, block in enumerate(
                    (jnp.where(first, mine, other), jnp.where(first, other, mine))
                ):
                    wq[:, side * q : (side + 1) * q] = block[:, :q]
                    wk[:, side * k : (side + 1) * k] = block[:, q : q + k]
                    wv[:, side * k : (side + 1) * k] = block[:, q + k : q + 2 * k]
                    for h in range(heads):
                        row = (side * heads + h) * HD
                        cut = q + 2 * k + h * tall
                        wo[row : row + HD] = block[:, cut : cut + tall]


def place_grads(meta, own, sib, shapes, pieces, into=()):
    tall = own[0].shape[-2]
    size = len(pieces)

    def spot(i, m):
        return (i // size) * 4 + (m[0] ^ (i % size + pieces[0]))

    rows = lambda s: pl.BlockSpec((tall, s[1]), lambda i, m: (spot(i, m), 0))
    specs = [rows(s) for s in shapes[:3]]
    specs.append(pl.BlockSpec((shapes[3][0], tall), lambda i, m: (0, spot(i, m))))
    inputs = 2 * len(own)
    return pl.pallas_call(
        functools.partial(place_kernel, tuple(pieces), len(own)),
        grid_spec=pltpu.PrefetchScalarGridSpec(
            num_scalar_prefetch=1,
            grid=(2 * size,),
            in_specs=[whole()] * inputs + [pl.BlockSpec(memory_space=pl.ANY)] * len(into),
            out_specs=specs,
        ),
        out_shape=[jax.ShapeDtypeStruct(s, jnp.float32) for s in shapes],
        input_output_aliases={1 + inputs + n: n for n in range(len(into))},
        compiler_params=params(LOW),
        cost_estimate=cost(0, size * 2 * sum(s[0] * s[1] for s in shapes)),
        name="place_grads",
    )(meta, *own, *sib, *into)


def context_part(meta, ref, j, quarter):
    side = ref.shape[1] // 2
    at = (meta[0] ^ j) * quarter
    head = ((at // side) ^ meta[1]) * side + at % side
    return ref[:, pl.ds(pl.multiple_of(head, quarter), quarter)]


def near_kernel(meta, tok_ref, *refs):
    contexts, own, sib, out_ref = refs[:3], refs[3:6], refs[6:9], refs[9]
    step = pl.program_id(0)
    quarter = own[0].shape[1]

    def run(group):
        for k, ref in enumerate(contexts):
            total = nn(context_part(meta, ref, 0, quarter), group[0][k])
            for j in range(1, 3):
                total += nn(context_part(meta, ref, j, quarter), group[j][k])
            if k == 0:
                out_ref[...] = tok_ref[...].astype(jnp.float32) + total
            else:
                out_ref[...] += total

    @pl.when(step == 0)
    def _():
        run(own)

    @pl.when(step == 1)
    def _():
        run(sib)


def output_near(meta, flat, contexts, own, sib):
    count = flat.shape[0]
    half = own[0].shape[2]
    wide = contexts[0].shape[1]
    return pl.pallas_call(
        near_kernel,
        grid_spec=pltpu.PrefetchScalarGridSpec(
            num_scalar_prefetch=1,
            grid=(2,),
            in_specs=[pl.BlockSpec((count, half), lambda i, m: (0, 2 * m[2] + (m[1] ^ i)))]
            + [whole()] * 9,
            out_specs=pl.BlockSpec((count, half), lambda i, m: (0, m[1] ^ i)),
        ),
        out_shape=jax.ShapeDtypeStruct((count, 2 * half), jnp.float32),
        compiler_params=params(LOW),
        cost_estimate=cost(12 * count * wide * half, 32 * wide * half),
        name="output_near",
    )(meta, flat, *contexts, *own[:3], *sib[:3])


def far_kernel(meta, sum_ref, c0, c1, c2, c3, *refs):
    own, sib, out_ref = refs[:5], refs[5:10], refs[10]
    step = pl.program_id(0)
    quarter = own[0].shape[1]

    def run(group):
        total = sum_ref[...]
        for k, ref in enumerate((c0, c1, c2, c3)):
            total += nn(context_part(meta, ref, 3, quarter), group[3 + k // 2][k % 2])
        for j in range(3):
            total += nn(context_part(meta, c3, j, quarter), group[j][0])
        out_ref[...] = total.astype(jnp.bfloat16)

    @pl.when(step == 0)
    def _():
        run(own)

    @pl.when(step == 1)
    def _():
        run(sib)


def output_far(meta, near, contexts, own, sib):
    count, columns = near.shape
    half = columns // 2
    quarter = own[0].shape[1]
    slots = [pl.BlockSpec((1, quarter, half), lambda i, m: (3, 0, 0))] * 3 + [whole()] * 2
    return pl.pallas_call(
        far_kernel,
        grid_spec=pltpu.PrefetchScalarGridSpec(
            num_scalar_prefetch=1,
            grid=(2,),
            in_specs=[pl.BlockSpec((count, half), lambda i, m: (0, m[1] ^ i))]
            + [whole()] * 4
            + slots * 2,
            out_specs=pl.BlockSpec((count, half), lambda i, m: (0, m[1] ^ i)),
        ),
        out_shape=jax.ShapeDtypeStruct((count, columns), jnp.bfloat16),
        compiler_params=params(LOW),
        cost_estimate=cost(4 * count * 7 * quarter * half, 8 * count * columns),
        name="output_far",
    )(meta, near, *contexts, *own, *sib)


def plane_body(
    prefix_tokens,
    prefix_len,
    causal_start,
    span_sample,
    bb_wq,
    bb_wk,
    bb_wv,
    bb_wo,
    action_tokens,
    ex_wq,
    ex_wk,
    ex_wv,
    ex_wo,
    action_cot,
):
    samples, positions, width = prefix_tokens.shape
    factor = 1.0 / math.sqrt(HD)
    count = samples * positions
    flat = prefix_tokens.reshape(count, width)
    device = lax.axis_index("dp")
    chip, core = device // 2, device % 2
    plane = lax.axis_index("tensor")

    def across(mask):
        return lambda x: lax.ppermute(x, "dp", [(i, i ^ mask) for i in range(8)])

    swap, over_x, over_y = across(1), across(2), across(4)

    def after(x, *others):
        return lax.optimization_barrier((x, *others))[0]

    local = jnp.concatenate([prefix_len, causal_start, span_sample])
    remote = swap(local)
    meta = jnp.concatenate(
        [
            jnp.stack([chip, core, plane, 0]).astype(jnp.int32),
            local[:2],
            remote[:2],
            local[2:4],
            remote[2:4],
            local[4:],
            remote[4:] + samples,
        ]
    )
    chip_meta = jnp.stack([chip, core, plane, 0]).astype(jnp.int32)

    def halves(weight):
        size = weight.shape[1] // 2
        mine = lax.dynamic_slice_in_dim(weight, core * size, size, 1)
        other = lax.dynamic_slice_in_dim(weight, (1 - core) * size, size, 1)
        return mine, other

    k_mine, k_other = halves(bb_wk)
    v_mine, v_other = halves(bb_wv)
    q_mine, q_other = halves(bb_wq)
    kv_got = swap(jnp.concatenate([k_other, v_other], axis=1))
    kv_shard = jnp.concatenate([jnp.concatenate([k_mine, v_mine], axis=1), kv_got])
    kv_x, kv_y = over_x(kv_shard), over_y(kv_shard)

    q_got = swap(after(q_other, kv_shard))
    spans = action_tokens.shape[0]
    pad = ((0, 0), (0, PAD - STEPS), (0, 0))
    pair = jnp.stack([jnp.pad(action_tokens, pad), jnp.pad(action_cot, pad)])
    pair = pair.reshape(2, spans * PAD, action_tokens.shape[2])
    pair_sib = swap(after(pair, kv_shard))
    normed = normalise(chip_meta, after(flat, q_other, pair), 4)
    normed_sib = swap(after(normed, kv_x, kv_y, q_got, pair_sib))
    half = kv_x.shape[0] // 2
    low, high = kv_y[:half], kv_x[half:]
    kv_dx, kv_dy = over_x(low), over_y(high)
    proj, dctx = expert_project(
        chip_meta, after(pair, low, high), pair_sib, ex_wq, ex_wk, ex_wv, ex_wo
    )
    q_shard = after(jnp.concatenate([q_mine, q_got]), kv_dx, kv_dy, normed_sib, proj)
    q_x, q_y = over_x(q_shard), over_y(q_shard)

    quarter = bb_wo.shape[0] // 4
    wo_rows = after(bb_wo, q_shard)
    by_chip = [
        lax.dynamic_slice_in_dim(wo_rows, (chip ^ m) * quarter, quarter, 0) for m in range(4)
    ]
    wo_a = [by_chip[0], over_x(by_chip[1]), over_y(by_chip[2]), across(6)(by_chip[3])]

    kv = project_kv(normed, normed_sib, (kv_shard, kv_x, kv_y, kv_dx, kv_dy))
    ectx, egrad = expert_attend(meta, proj, dctx, kv, factor)
    low, high = after(q_y, ectx, *wo_a)[:half], after(q_x, ectx, *wo_a)[half:]
    q_dx, q_dy = over_x(low), over_y(high)
    wo_a = jnp.stack(wo_a)
    wo_b = []
    for s in range(4):
        piece = lax.dynamic_index_in_dim(
            wo_a, chip ^ lax.rem(plane + s, 4), 0, keepdims=False
        )
        perm = [(i, (i + s) % 4) for i in range(4)]
        wo_b.append(lax.ppermute(piece, "tensor", perm) if s else piece)

    ax, ak, by, bk = weight_grads(chip_meta, pair, pair_sib, after(ectx, low, high), egrad)
    a_got, b_got = over_x(ax), over_y(by)
    ctx = attend(
        meta, normed, normed_sib, (q_shard, q_x, q_y, q_dx, q_dy), after(kv, ax), positions, factor
    )
    ctx_own, ctx_other = ctx
    wo_b = [after(x, ctx_own) for x in wo_b]
    a_got, b_got = after(a_got, ctx_own), after(b_got, ctx_own)
    ctx_got = swap(after(ctx_other, a_got, b_got, *wo_b))
    ctx_rows = jnp.concatenate([ctx_own, ctx_got], axis=1)
    turn = lambda x: lax.ppermute(x, "tensor", [(i, (i + 1) % 4) for i in range(4)])
    ctx_1 = turn(ctx_rows)
    a_sum, b_sum = ak + a_got, bk + b_got
    a_rest, b_rest = over_y(a_sum[1]), over_x(b_sum[1])
    mine = jnp.stack([a_sum[0] + a_rest, b_sum[0] + b_rest])
    wo = after(jnp.stack([after(x, ctx_got) for x in wo_b]), a_rest, b_rest)
    wo_x, wo_y = over_x(wo), over_y(wo)
    sent = after(mine, wo_x, wo_y)
    from_x, from_y = over_x(sent), over_y(sent)
    ctx_2 = turn(ctx_1)
    wo_sib = [swap(after(wo, wo_x)), swap(wo_x), swap(wo_y)]
    wo_dx = over_x(after(wo_y, from_x, from_y, wo_sib[0])[:2])
    wo_dy = over_y(after(wo_x, from_x, from_y, wo_sib[0])[2:])
    ctx_3 = turn(ctx_2)
    near = output_near(chip_meta, flat, (ctx_rows, ctx_1, ctx_2), (wo, wo_x, wo_y), wo_sib)
    far_x = over_x(after(from_y, wo_dx, wo_dy)[0])
    far_y = over_y(after(from_x, wo_dx, wo_dy)[1])
    near_grads = (mine, from_x, from_y)
    near_sib = tuple(swap(x) for x in near_grads)
    shapes = (ex_wq.shape, ex_wk.shape, ex_wv.shape, ex_wo.shape)
    grads = place_grads(chip_meta, near_grads, near_sib, shapes, range(3))
    wo_own = (wo, wo_x, wo_y, wo_dx, wo_dy)
    wo_sib += [swap(wo_dx), swap(wo_dy)]
    far = (far_x, far_y)
    grads = place_grads(chip_meta, far, [swap(x) for x in far], shapes, range(3, 4), grads)
    out = output_far(chip_meta, near, (ctx_rows, ctx_1, ctx_2, ctx_3), wo_own, wo_sib)
    return (out.reshape(samples, positions, -1), *grads)


def fits_plane(mesh):
    return mesh.shape["dp"] == 8 and mesh.shape["tensor"] == 4


def solution(mesh):
    in_specs = (
        P("dp", None, None),
        P("dp"),
        P("dp"),
        P("dp"),
        P("dp", "tensor"),
        P("dp", "tensor"),
        P("dp", "tensor"),
        P("tensor", "dp"),
        P("dp", None, None),
        P(None, "tensor"),
        P(None, "tensor"),
        P(None, "tensor"),
        P("tensor", None),
        P("dp", None, None),
    )
    out_specs = (
        P("dp", None, "tensor"),
        P(None, "tensor"),
        P(None, "tensor"),
        P(None, "tensor"),
        P("tensor", None),
    )
    body = plane_body if fits_plane(mesh) else general_body
    return jax.shard_map(body, mesh=mesh, in_specs=in_specs, out_specs=out_specs, check_vma=False)
```

```python
import functools
import math

import jax
import jax.numpy as jnp
from jax import lax
from jax.experimental import pallas as pl
from jax.experimental.pallas import tpu as pltpu
from jax.sharding import PartitionSpec as P

HD = 128
STEPS = 50


def general_body(
    prefix_tokens,
    prefix_len,
    causal_start,
    span_sample,
    bb_wq,
    bb_wk,
    bb_wv,
    bb_wo,
    action_tokens,
    ex_wq,
    ex_wk,
    ex_wv,
    ex_wo,
    action_cot,
):
    samples, positions, width = prefix_tokens.shape
    factor = 1.0 / math.sqrt(HD)
    kv_local = bb_wk.shape[1] // HD
    group = bb_wq.shape[1] // bb_wk.shape[1]
    egroup = ex_wq.shape[1] // ex_wk.shape[1]
    count = samples * positions
    flat = prefix_tokens.reshape(count, width)
    widened = flat.astype(jnp.float32)
    normed = (
        widened * lax.rsqrt(jnp.mean(widened * widened, axis=-1, keepdims=True) + 1e-06)
    ).astype(jnp.bfloat16)
    pieces = (
        lax.all_gather(bb_wq, "dp", axis=0, tiled=True),
        lax.all_gather(bb_wk, "dp", axis=0, tiled=True),
        lax.all_gather(bb_wv, "dp", axis=0, tiled=True),
    )
    query_sum, key_sum, value_sum = tuple(
        (jnp.dot(normed, piece, preferred_element_type=jnp.float32) for piece in pieces)
    )
    query = query_sum.astype(jnp.bfloat16).reshape(samples, positions, kv_local, group, HD)
    keys = key_sum.astype(jnp.bfloat16).reshape(samples, positions, kv_local, HD)
    values = value_sum.astype(jnp.bfloat16).reshape(samples, positions, kv_local, HD)
    scores = (
        jnp.einsum("sigeh,sjgh->sgeij", query, keys, preferred_element_type=jnp.float32) * factor
    )
    places = jnp.arange(positions, dtype=jnp.int32)
    length_view = prefix_len[:, None, None, None, None]
    start_view = causal_start[:, None, None, None, None]
    visible = (places[None, None, None, None, :] < length_view) & (
        (places[None, None, None, None, :] < start_view)
        | (places[None, None, None, None, :] <= places[None, None, None, :, None])
    )
    scores = jnp.where(visible, scores, -1e30)
    top = jnp.max(scores, axis=-1, keepdims=True)
    weights = jnp.where(visible, jnp.exp(scores - top), 0.0)
    weights = (weights / jnp.sum(weights, axis=-1, keepdims=True)).astype(jnp.bfloat16)
    context = (
        jnp.einsum("sgeij,sjgh->sigeh", weights, values, preferred_element_type=jnp.float32)
        .astype(jnp.bfloat16)
        .reshape(count, bb_wq.shape[1])
    )
    partial_out = jnp.dot(
        context, lax.all_gather(bb_wo, "dp", axis=1, tiled=True), preferred_element_type=jnp.float32
    )
    summed = lax.psum_scatter(partial_out, "tensor", scatter_dimension=1, tiled=True)
    share = summed.shape[1]
    residual = lax.dynamic_slice_in_dim(widened, lax.axis_index("tensor") * share, share, 1)
    prefix_out = (residual + summed).astype(jnp.bfloat16).reshape(samples, positions, share)
    spans = action_tokens.shape[0]
    rows = spans * STEPS
    action_flat = action_tokens.reshape(rows, action_tokens.shape[2])
    cot_flat = action_cot.reshape(rows, action_cot.shape[2])
    pre_keys = jnp.take(keys, span_sample, axis=0)
    pre_values = jnp.take(values, span_sample, axis=0)
    span_length = jnp.take(prefix_len, span_sample, axis=0)
    equery = (
        jnp.dot(action_flat, ex_wq, preferred_element_type=jnp.float32)
        .astype(jnp.bfloat16)
        .reshape(spans, STEPS, kv_local, egroup, HD)
    )
    own_keys = (
        jnp.dot(action_flat, ex_wk, preferred_element_type=jnp.float32)
        .astype(jnp.bfloat16)
        .reshape(spans, STEPS, kv_local, HD)
    )
    own_values = (
        jnp.dot(action_flat, ex_wv, preferred_element_type=jnp.float32)
        .astype(jnp.bfloat16)
        .reshape(spans, STEPS, kv_local, HD)
    )
    valid = (places[None, :] < span_length[:, None])[:, None, None, None, :]
    score_pre = (
        jnp.einsum("ctgeh,cpgh->cgetp", equery, pre_keys, preferred_element_type=jnp.float32)
        * factor
    )
    score_pre = jnp.where(valid, score_pre, -1e30)
    score_own = (
        jnp.einsum("ctgeh,cugh->cgetu", equery, own_keys, preferred_element_type=jnp.float32)
        * factor
    )
    peak = jnp.maximum(jnp.max(score_pre, axis=-1), jnp.max(score_own, axis=-1))[..., None]
    exp_pre = jnp.where(valid, jnp.exp(score_pre - peak), 0.0)
    exp_own = jnp.exp(score_own - peak)
    total = jnp.sum(exp_pre, axis=-1, keepdims=True) + jnp.sum(exp_own, axis=-1, keepdims=True)
    prob_pre = exp_pre / total
    prob_own = exp_own / total
    half_pre = prob_pre.astype(jnp.bfloat16)
    half_own = prob_own.astype(jnp.bfloat16)
    econtext = (
        jnp.einsum("cgetp,cpgh->ctgeh", half_pre, pre_values, preferred_element_type=jnp.float32)
        + jnp.einsum("cgetu,cugh->ctgeh", half_own, own_values, preferred_element_type=jnp.float32)
    ).astype(jnp.bfloat16)
    econtext_flat = econtext.reshape(rows, ex_wq.shape[1])
    grad_out_local = jnp.einsum(
        "ti,tj->ij", econtext_flat, cot_flat, preferred_element_type=jnp.float32
    )
    dcontext = (
        jnp.einsum("tj,ij->ti", cot_flat, ex_wo, preferred_element_type=jnp.float32)
        .astype(jnp.bfloat16)
        .reshape(spans, STEPS, kv_local, egroup, HD)
    )
    dprob_pre = jnp.einsum(
        "ctgeh,cpgh->cgetp", dcontext, pre_values, preferred_element_type=jnp.float32
    )
    dprob_own = jnp.einsum(
        "ctgeh,cugh->cgetu", dcontext, own_values, preferred_element_type=jnp.float32
    )
    delta = (jnp.sum(prob_pre * dprob_pre, axis=-1) + jnp.sum(prob_own * dprob_own, axis=-1))[
        ..., None
    ]
    dscore_pre = (prob_pre * (dprob_pre - delta) * factor).astype(jnp.bfloat16)
    dscore_own = (prob_own * (dprob_own - delta) * factor).astype(jnp.bfloat16)
    dquery = (
        jnp.einsum("cgetp,cpgh->ctgeh", dscore_pre, pre_keys, preferred_element_type=jnp.float32)
        + jnp.einsum("cgetu,cugh->ctgeh", dscore_own, own_keys, preferred_element_type=jnp.float32)
    ).astype(jnp.bfloat16)
    dkeys = jnp.einsum(
        "cgetu,ctgeh->cugh", dscore_own, equery, preferred_element_type=jnp.float32
    ).astype(jnp.bfloat16)
    dvalues = jnp.einsum(
        "cgetu,ctgeh->cugh", half_own, dcontext, preferred_element_type=jnp.float32
    ).astype(jnp.bfloat16)
    grad_query_local = jnp.einsum(
        "ti,tj->ij",
        action_flat,
        dquery.reshape(rows, ex_wq.shape[1]),
        preferred_element_type=jnp.float32,
    )
    grad_key_local = jnp.einsum(
        "ti,tj->ij",
        action_flat,
        dkeys.reshape(rows, ex_wk.shape[1]),
        preferred_element_type=jnp.float32,
    )
    grad_value_local = jnp.einsum(
        "ti,tj->ij",
        action_flat,
        dvalues.reshape(rows, ex_wv.shape[1]),
        preferred_element_type=jnp.float32,
    )
    grad_wq, grad_wk, grad_wv, grad_wo = lax.psum(
        (grad_query_local, grad_key_local, grad_value_local, grad_out_local), "dp"
    )
    return (prefix_out, grad_wq, grad_wk, grad_wv, grad_wo)


NEG = -1e30
PAD = 64
HIGH = 56 * 1024 * 1024
LOW = 32 * 1024 * 1024


def params(limit=HIGH):
    return pltpu.CompilerParams(vmem_limit_bytes=limit)


def cost(flops, moved):
    return pl.CostEstimate(flops=int(flops), bytes_accessed=int(moved), transcendentals=0)


def whole():
    return pl.BlockSpec(memory_space=pltpu.VMEM)


def nt(a, b):
    return lax.dot_general(a, b, (((1,), (1,)), ((), ())), preferred_element_type=jnp.float32)


def tn(a, b):
    return lax.dot_general(a, b, (((0,), (0,)), ((), ())), preferred_element_type=jnp.float32)


def nn(a, b):
    return jnp.dot(a, b, preferred_element_type=jnp.float32)


def norm_kernel(meta, x_ref, out_ref):
    chip, core = meta[0], meta[1]
    parts, rows, wide = out_ref.shape
    half = wide // 2
    x = x_ref[...].astype(jnp.float32)
    scale = lax.rsqrt(jnp.mean(x * x, axis=-1, keepdims=True) + 1e-06)
    for j in range(parts):
        for side in range(2):
            at = pl.multiple_of(((chip ^ j) * 2 + (core ^ side)) * half, half)
            piece = x_ref[:, pl.ds(at, half)].astype(jnp.float32)
            out_ref[j, :, side * half : (side + 1) * half] = (piece * scale).astype(jnp.bfloat16)


def normalise(meta, flat, parts):
    count, width = flat.shape
    block = 128
    return pl.pallas_call(
        norm_kernel,
        grid_spec=pltpu.PrefetchScalarGridSpec(
            num_scalar_prefetch=1,
            grid=(count // block,),
            in_specs=[pl.BlockSpec((block, width), lambda i, m: (i, 0))],
            out_specs=pl.BlockSpec((parts, block, width // parts), lambda i, m: (0, i, 0)),
        ),
        out_shape=jax.ShapeDtypeStruct((parts, count, width // parts), jnp.bfloat16),
        compiler_params=params(),
        cost_estimate=cost(4 * count * width, 4 * count * width),
        name="normalise",
    )(meta, flat)


def product(ref, weights, swapped):
    w0, w1, w2, wx, wy = weights
    half = wx.shape[0]
    first, second = slice(0, half), slice(half, 2 * half)
    if not swapped:
        total = nn(ref[0], w0[...]) + nn(ref[1], w1[...]) + nn(ref[2], w2[...])
        return total + nn(ref[3, :, first], wx[...]) + nn(ref[3, :, second], wy[...])
    total = nn(ref[3, :, second], wx[...]) + nn(ref[3, :, first], wy[...])
    for j, weight in enumerate((w0, w1, w2)):
        total += nn(ref[j, :, second], weight[first]) + nn(ref[j, :, first], weight[second])
    return total


def kv_kernel(own_ref, sib_ref, w0, w1, w2, wx, wy, out_ref):
    step = pl.program_id(0)
    half = pl.num_programs(0) // 2
    weights = (w0, w1, w2, wx, wy)

    @pl.when(step < half)
    def _():
        out_ref[...] = product(own_ref, weights, False).astype(jnp.bfloat16)

    @pl.when(step >= half)
    def _():
        out_ref[...] = product(sib_ref, weights, True).astype(jnp.bfloat16)


def pair_specs(parts, block, wide, steps, sib_first=False):
    first = pl.BlockSpec(
        (parts, block, wide), lambda i, *m: (0, jnp.minimum(i, steps // 2 - 1), 0)
    )
    then = pl.BlockSpec((parts, block, wide), lambda i, *m: (0, jnp.maximum(i - steps // 2, 0), 0))
    return [then, first] if sib_first else [first, then]


def project_kv(own, sib, weights):
    parts, count, wide = own.shape
    columns = weights[0].shape[1]
    block = 256
    steps = 2 * count // block
    return pl.pallas_call(
        kv_kernel,
        grid=(steps,),
        in_specs=pair_specs(parts, block, wide, steps) + [whole()] * 5,
        out_specs=pl.BlockSpec((block, columns), lambda i: (i, 0)),
        out_shape=jax.ShapeDtypeStruct((2 * count, columns), jnp.bfloat16),
        compiler_params=params(),
        cost_estimate=cost(4 * count * parts * wide * columns, 4 * count * parts * wide),
        name="project_kv",
    )(own, sib, *weights)


def attend_kernel(factor, meta, own_ref, sib_ref, w0, w1, w2, wx, wy, kv_ref, own_out, sib_out, query, context):
    step = pl.program_id(0)
    half = pl.num_programs(0) // 2
    weights = (w0, w1, w2, wx, wy)

    @pl.when(step >= half)
    def _():
        query[...] = product(own_ref, weights, False).astype(jnp.bfloat16)

    @pl.when(step < half)
    def _():
        query[...] = product(sib_ref, weights, True).astype(jnp.bfloat16)

    sample = lax.rem(step + half, 2 * half)
    length = meta[4 + sample]
    start = meta[8 + sample]
    positions = context.shape[0]
    keys = kv_ref[:, :HD]
    values = kv_ref[:, HD:]
    row = lax.broadcasted_iota(jnp.int32, (positions, positions), 0)
    column = lax.broadcasted_iota(jnp.int32, (positions, positions), 1)
    visible = (column < length) & ((column < start) | (column <= row))
    for head in range(context.shape[1] // HD):
        at = slice(head * HD, (head + 1) * HD)
        scores = jnp.where(visible, nt(query[:, at], keys) * factor, NEG)
        top = jnp.max(scores, axis=-1, keepdims=True)
        weight = jnp.where(visible, jnp.exp(scores - top), 0.0)
        weight = (weight / jnp.sum(weight, axis=-1, keepdims=True)).astype(jnp.bfloat16)
        context[:, at] = nn(weight, values).astype(jnp.bfloat16)

    @pl.when(step >= half)
    def _():
        own_out[...] = context[...]

    @pl.when(step < half)
    def _():
        sib_out[...] = context[...]


def attend(meta, own, sib, weights, kv, positions, factor):
    parts, count, wide = own.shape
    columns = weights[0].shape[1]
    steps = 2 * count // positions
    half = steps // 2
    out = jax.ShapeDtypeStruct((count, columns), jnp.bfloat16)
    return pl.pallas_call(
        functools.partial(attend_kernel, factor),
        grid_spec=pltpu.PrefetchScalarGridSpec(
            num_scalar_prefetch=1,
            grid=(steps,),
            in_specs=pair_specs(parts, positions, wide, steps, True)
            + [whole()] * 5
            + [pl.BlockSpec((positions, 2 * HD), lambda i, m: ((i + half) % steps, 0))],
            out_specs=[
                pl.BlockSpec((positions, columns), lambda i, m: (jnp.maximum(i - half, 0), 0)),
                pl.BlockSpec((positions, columns), lambda i, m: (jnp.minimum(i, half - 1), 0)),
            ],
            scratch_shapes=[pltpu.VMEM((positions, columns), jnp.bfloat16)] * 2,
        ),
        out_shape=[out, out],
        compiler_params=params(),
        cost_estimate=cost(8 * count * parts * wide * columns, 4 * count * parts * wide),
        name="attend",
    )(meta, own, sib, *weights, kv)


def expert_project_kernel(meta, own_ref, sib_ref, wq, wk, wv, wo, out_ref, cot_ref):
    step = pl.program_id(0)
    half = pl.num_programs(0) // 2

    def run(ref):
        action = ref[0]
        q, k = wq.shape[1], wk.shape[1]
        out_ref[:, :q] = nn(action, wq[...]).astype(jnp.bfloat16)
        out_ref[:, q : q + k] = nn(action, wk[...]).astype(jnp.bfloat16)
        out_ref[:, q + k :] = nn(action, wv[...]).astype(jnp.bfloat16)
        cot_ref[...] = nt(ref[1], wo[...]).astype(jnp.bfloat16)

    @pl.when(step < half)
    def _():
        run(own_ref)

    @pl.when(step >= half)
    def _():
        run(sib_ref)


def expert_project(meta, own, sib, wq, wk, wv, wo):
    _, rows, width = own.shape
    block = 256
    steps = 2 * rows // block
    q, k = wq.shape[1] // 2, wk.shape[1] // 2
    return pl.pallas_call(
        expert_project_kernel,
        grid_spec=pltpu.PrefetchScalarGridSpec(
            num_scalar_prefetch=1,
            grid=(steps,),
            in_specs=pair_specs(2, block, width, steps)
            + [
                pl.BlockSpec((width, q), lambda i, m: (0, m[1])),
                pl.BlockSpec((width, k), lambda i, m: (0, m[1])),
                pl.BlockSpec((width, k), lambda i, m: (0, m[1])),
                pl.BlockSpec((q, width), lambda i, m: (m[1], 0)),
            ],
            out_specs=[
                pl.BlockSpec((block, q + 2 * k), lambda i, m: (i, 0)),
                pl.BlockSpec((block, q), lambda i, m: (i, 0)),
            ],
        ),
        out_shape=[
            jax.ShapeDtypeStruct((2 * rows, q + 2 * k), jnp.bfloat16),
            jax.ShapeDtypeStruct((2 * rows, q), jnp.bfloat16),
        ],
        compiler_params=params(),
        cost_estimate=cost(4 * rows * width * (2 * q + 2 * k), 8 * rows * width),
        name="expert_project",
    )(meta, own, sib, wq, wk, wv, wo)


def expert_kernel(factor, spans, meta, proj_ref, dctx_ref, kv_ref, ctx_ref, grad_ref):
    step = pl.program_id(0)
    positions = meta.shape[0] and 256
    width = dctx_ref.shape[1]
    heads = width // HD
    rows = heads * PAD
    own_column = lax.broadcasted_iota(jnp.int32, (rows, PAD), 1)
    pre_column = lax.broadcasted_iota(jnp.int32, (rows, positions), 1)
    for s in range(spans):
        sample = meta[12 + step * spans + s]
        valid = pre_column < meta[4 + sample]
        own_valid = own_column < STEPS
        at = slice(s * PAD, (s + 1) * PAD)
        base = pl.multiple_of(sample * positions, positions)
        pre_keys = kv_ref[pl.ds(base, positions), :HD]
        pre_values = kv_ref[pl.ds(base, positions), HD:]
        stack = lambda ref: jnp.concatenate(
            [ref[at, h * HD : (h + 1) * HD] for h in range(heads)], axis=0
        )
        query = stack(proj_ref)
        cot = stack(dctx_ref)
        own_keys = proj_ref[at, width : width + HD]
        own_values = proj_ref[at, width + HD :]
        score_pre = jnp.where(valid, nt(query, pre_keys) * factor, NEG)
        score_own = jnp.where(own_valid, nt(query, own_keys) * factor, NEG)
        peak = jnp.maximum(
            jnp.max(score_pre, axis=-1, keepdims=True), jnp.max(score_own, axis=-1, keepdims=True)
        )
        exp_pre = jnp.where(valid, jnp.exp(score_pre - peak), 0.0)
        exp_own = jnp.where(own_valid, jnp.exp(score_own - peak), 0.0)
        total = jnp.sum(exp_pre, axis=-1, keepdims=True) + jnp.sum(exp_own, axis=-1, keepdims=True)
        prob_pre = exp_pre / total
        prob_own = exp_own / total
        half_pre = prob_pre.astype(jnp.bfloat16)
        half_own = prob_own.astype(jnp.bfloat16)
        context = (nn(half_pre, pre_values) + nn(half_own, own_values)).astype(jnp.bfloat16)
        dprob_pre = nt(cot, pre_values)
        dprob_own = nt(cot, own_values)
        delta = jnp.sum(prob_pre * dprob_pre, axis=-1, keepdims=True) + jnp.sum(
            prob_own * dprob_own, axis=-1, keepdims=True
        )
        dscore_pre = (prob_pre * (dprob_pre - delta) * factor).astype(jnp.bfloat16)
        dscore_own = (prob_own * (dprob_own - delta) * factor).astype(jnp.bfloat16)
        dquery = (nn(dscore_pre, pre_keys) + nn(dscore_own, own_keys)).astype(jnp.bfloat16)
        for h in range(heads):
            part = slice(h * PAD, (h + 1) * PAD)
            ctx_ref[at, h * HD : (h + 1) * HD] = context[part]
            grad_ref[at, h * HD : (h + 1) * HD] = dquery[part]
        grad_ref[at, width : width + HD] = tn(dscore_own, query).astype(jnp.bfloat16)
        grad_ref[at, width + HD :] = tn(half_own, cot).astype(jnp.bfloat16)


def expert_attend(meta, proj, dctx, kv, factor):
    rows, columns = proj.shape
    width = dctx.shape[1]
    spans = 4
    steps = rows // (PAD * spans)
    block = PAD * spans
    return pl.pallas_call(
        functools.partial(expert_kernel, factor, spans),
        grid_spec=pltpu.PrefetchScalarGridSpec(
            num_scalar_prefetch=1,
            grid=(steps,),
            in_specs=[
                pl.BlockSpec((block, columns), lambda i, m: (i, 0)),
                pl.BlockSpec((block, width), lambda i, m: (i, 0)),
                whole(),
            ],
            out_specs=[
                pl.BlockSpec((block, width), lambda i, m: (i, 0)),
                pl.BlockSpec((block, columns), lambda i, m: (i, 0)),
            ],
        ),
        out_shape=[
            jax.ShapeDtypeStruct((rows, width), jnp.bfloat16),
            jax.ShapeDtypeStruct((rows, columns), jnp.bfloat16),
        ],
        compiler_params=params(LOW),
        cost_estimate=cost(40 * rows * 320 * width, 8 * rows * columns),
        name="expert_attend",
    )(meta, proj, dctx, kv)


def grads_kernel(meta, own_ref, sib_ref, ctx_ref, grad_ref, ax_ref, ak_ref, by_ref, bk_ref):
    chip = meta[0]
    step = pl.program_id(0)
    rows = own_ref.shape[1]
    tall = ax_ref.shape[1]
    wide = grad_ref.shape[1]
    heads = ctx_ref.shape[1] // HD

    def piece(route, j, ref):
        at = pl.ds(pl.multiple_of((route * 4 + (chip ^ j)) * tall, tall), tall)
        ref[0, :, :wide] = tn(own_ref[0, :, at], grad_ref[:rows]) + tn(
            sib_ref[0, :, at], grad_ref[rows:]
        )
        for h in range(heads):
            cut = slice(h * HD, (h + 1) * HD)
            ref[0, :, wide + h * tall : wide + (h + 1) * tall] = tn(
                ctx_ref[:rows, cut], own_ref[1, :, at]
            ) + tn(ctx_ref[rows:, cut], sib_ref[1, :, at])

    piece(0, 1 + 2 * step, ax_ref)
    piece(1, 2 + step, by_ref)
    piece(0, 2 * step, ak_ref)
    piece(1, step, bk_ref)


def weight_grads(meta, own, sib, ctx, grad):
    _, rows, width = own.shape
    tall = width // 8
    columns = grad.shape[1] + ctx.shape[1] // HD * tall
    out = jax.ShapeDtypeStruct((2, tall, columns), jnp.float32)
    return pl.pallas_call(
        grads_kernel,
        grid_spec=pltpu.PrefetchScalarGridSpec(
            num_scalar_prefetch=1,
            grid=(2,),
            in_specs=[whole()] * 4,
            out_specs=[pl.BlockSpec((1, tall, columns), lambda i, m: (i, 0, 0))] * 4,
        ),
        out_shape=[out] * 4,
        compiler_params=params(LOW),
        cost_estimate=cost(4 * rows * width * columns, 16 * width * columns),
        name="weight_grads",
    )(meta, own, sib, ctx, grad)


def place_kernel(pieces, groups, meta, *refs):
    own, sib, outs = refs[:groups], refs[groups : 2 * groups], refs[-4:]
    step = pl.program_id(0)
    first = meta[1] == 0
    wq, wk, wv, wo = outs
    tall = wq.shape[0]
    q, k = wq.shape[1] // 2, wk.shape[1] // 2
    heads = wo.shape[0] // (2 * HD)

    def pick(group, route, j):
        if j < 3:
            return group[j][route]
        return group[route][...]

    for route in range(2):
        for place, j in enumerate(pieces):

            @pl.when(step == route * len(pieces) + place)
            def _():
                mine, other = pick(own, route, j), pick(sib, route, j)
                for side, block in enumerate(
                    (jnp.where(first, mine, other), jnp.where(first, other, mine))
                ):
                    wq[:, side * q : (side + 1) * q] = block[:, :q]
                    wk[:, side * k : (side + 1) * k] = block[:, q : q + k]
                    wv[:, side * k : (side + 1) * k] = block[:, q + k : q + 2 * k]
                    for h in range(heads):
                        row = (side * heads + h) * HD
                        cut = q + 2 * k + h * tall
                        wo[row : row + HD] = block[:, cut : cut + tall]


def place_grads(meta, own, sib, shapes, pieces, into=()):
    tall = own[0].shape[-2]
    size = len(pieces)

    def spot(i, m):
        return (i // size) * 4 + (m[0] ^ (i % size + pieces[0]))

    rows = lambda s: pl.BlockSpec((tall, s[1]), lambda i, m: (spot(i, m), 0))
    specs = [rows(s) for s in shapes[:3]]
    specs.append(pl.BlockSpec((shapes[3][0], tall), lambda i, m: (0, spot(i, m))))
    inputs = 2 * len(own)
    return pl.pallas_call(
        functools.partial(place_kernel, tuple(pieces), len(own)),
        grid_spec=pltpu.PrefetchScalarGridSpec(
            num_scalar_prefetch=1,
            grid=(2 * size,),
            in_specs=[whole()] * inputs + [pl.BlockSpec(memory_space=pl.ANY)] * len(into),
            out_specs=specs,
        ),
        out_shape=[jax.ShapeDtypeStruct(s, jnp.float32) for s in shapes],
        input_output_aliases={1 + inputs + n: n for n in range(len(into))},
        compiler_params=params(LOW),
        cost_estimate=cost(0, size * 2 * sum(s[0] * s[1] for s in shapes)),
        name="place_grads",
    )(meta, *own, *sib, *into)


def context_part(meta, ref, j, quarter):
    side = ref.shape[1] // 2
    at = (meta[0] ^ j) * quarter
    head = ((at // side) ^ meta[1]) * side + at % side
    return ref[:, pl.ds(pl.multiple_of(head, quarter), quarter)]


def near_kernel(meta, tok_ref, *refs):
    contexts, own, sib, out_ref = refs[:3], refs[3:6], refs[6:9], refs[9]
    step = pl.program_id(0)
    quarter = own[0].shape[1]

    def run(group):
        for k, ref in enumerate(contexts):
            total = nn(context_part(meta, ref, 0, quarter), group[0][k])
            for j in range(1, 3):
                total += nn(context_part(meta, ref, j, quarter), group[j][k])
            if k == 0:
                out_ref[...] = tok_ref[...].astype(jnp.float32) + total
            else:
                out_ref[...] += total

    @pl.when(step == 0)
    def _():
        run(own)

    @pl.when(step == 1)
    def _():
        run(sib)


def output_near(meta, flat, contexts, own, sib):
    count = flat.shape[0]
    half = own[0].shape[2]
    wide = contexts[0].shape[1]
    return pl.pallas_call(
        near_kernel,
        grid_spec=pltpu.PrefetchScalarGridSpec(
            num_scalar_prefetch=1,
            grid=(2,),
            in_specs=[pl.BlockSpec((count, half), lambda i, m: (0, 2 * m[2] + (m[1] ^ i)))]
            + [whole()] * 9,
            out_specs=pl.BlockSpec((count, half), lambda i, m: (0, m[1] ^ i)),
        ),
        out_shape=jax.ShapeDtypeStruct((count, 2 * half), jnp.float32),
        compiler_params=params(LOW),
        cost_estimate=cost(12 * count * wide * half, 32 * wide * half),
        name="output_near",
    )(meta, flat, *contexts, *own[:3], *sib[:3])


def far_kernel(meta, sum_ref, c0, c1, c2, c3, *refs):
    own, sib, out_ref = refs[:5], refs[5:10], refs[10]
    step = pl.program_id(0)
    quarter = own[0].shape[1]

    def run(group):
        total = sum_ref[...]
        for k, ref in enumerate((c0, c1, c2, c3)):
            total += nn(context_part(meta, ref, 3, quarter), group[3 + k // 2][k % 2])
        for j in range(3):
            total += nn(context_part(meta, c3, j, quarter), group[j][0])
        out_ref[...] = total.astype(jnp.bfloat16)

    @pl.when(step == 0)
    def _():
        run(own)

    @pl.when(step == 1)
    def _():
        run(sib)


def output_far(meta, near, contexts, own, sib):
    count, columns = near.shape
    half = columns // 2
    quarter = own[0].shape[1]
    slots = [pl.BlockSpec((1, quarter, half), lambda i, m: (3, 0, 0))] * 3 + [whole()] * 2
    return pl.pallas_call(
        far_kernel,
        grid_spec=pltpu.PrefetchScalarGridSpec(
            num_scalar_prefetch=1,
            grid=(2,),
            in_specs=[pl.BlockSpec((count, half), lambda i, m: (0, m[1] ^ i))]
            + [whole()] * 4
            + slots * 2,
            out_specs=pl.BlockSpec((count, half), lambda i, m: (0, m[1] ^ i)),
        ),
        out_shape=jax.ShapeDtypeStruct((count, columns), jnp.bfloat16),
        compiler_params=params(LOW),
        cost_estimate=cost(4 * count * 7 * quarter * half, 8 * count * columns),
        name="output_far",
    )(meta, near, *contexts, *own, *sib)


def plane_body(
    prefix_tokens,
    prefix_len,
    causal_start,
    span_sample,
    bb_wq,
    bb_wk,
    bb_wv,
    bb_wo,
    action_tokens,
    ex_wq,
    ex_wk,
    ex_wv,
    ex_wo,
    action_cot,
):
    samples, positions, width = prefix_tokens.shape
    factor = 1.0 / math.sqrt(HD)
    count = samples * positions
    flat = prefix_tokens.reshape(count, width)
    device = lax.axis_index("dp")
    chip, core = device // 2, device % 2
    plane = lax.axis_index("tensor")

    def across(mask):
        return lambda x: lax.ppermute(x, "dp", [(i, i ^ mask) for i in range(8)])

    swap, over_x, over_y = across(1), across(2), across(4)

    def after(x, *others):
        return lax.optimization_barrier((x, *others))[0]

    local = jnp.concatenate([prefix_len, causal_start, span_sample])
    remote = swap(local)
    meta = jnp.concatenate(
        [
            jnp.stack([chip, core, plane, 0]).astype(jnp.int32),
            local[:2],
            remote[:2],
            local[2:4],
            remote[2:4],
            local[4:],
            remote[4:] + samples,
        ]
    )
    chip_meta = jnp.stack([chip, core, plane, 0]).astype(jnp.int32)

    def halves(weight):
        size = weight.shape[1] // 2
        mine = lax.dynamic_slice_in_dim(weight, core * size, size, 1)
        other = lax.dynamic_slice_in_dim(weight, (1 - core) * size, size, 1)
        return mine, other

    k_mine, k_other = halves(bb_wk)
    v_mine, v_other = halves(bb_wv)
    kv_got = swap(jnp.concatenate([k_other, v_other], axis=1))
    kv_shard = jnp.concatenate([jnp.concatenate([k_mine, v_mine], axis=1), kv_got])
    kv_x, kv_y = over_x(kv_shard), over_y(kv_shard)

    spans = action_tokens.shape[0]
    pad = ((0, 0), (0, PAD - STEPS), (0, 0))
    pair = jnp.stack([jnp.pad(action_tokens, pad), jnp.pad(action_cot, pad)])
    pair = pair.reshape(2, spans * PAD, action_tokens.shape[2])
    pair_sib = swap(after(pair, kv_shard))
    normed = normalise(chip_meta, after(flat, kv_shard, pair), 4)
    q_mine, q_other = halves(after(bb_wq, normed))
    q_got = swap(q_other)
    normed_sib = swap(after(normed, kv_x, kv_y, q_got, pair_sib))
    half = kv_x.shape[0] // 2
    low, high = kv_y[:half], kv_x[half:]
    kv_dx, kv_dy = over_x(low), over_y(high)
    proj, dctx = expert_project(
        chip_meta, after(pair, low, high), pair_sib, ex_wq, ex_wk, ex_wv, ex_wo
    )
    q_shard = after(jnp.concatenate([q_mine, q_got]), kv_dx, kv_dy, normed_sib, proj)
    q_x, q_y = over_x(q_shard), over_y(q_shard)

    quarter = bb_wo.shape[0] // 4
    wo_rows = after(bb_wo, q_shard)
    by_chip = [
        lax.dynamic_slice_in_dim(wo_rows, (chip ^ m) * quarter, quarter, 0) for m in range(4)
    ]
    wo_a = [by_chip[0], over_x(by_chip[1]), over_y(by_chip[2]), across(6)(by_chip[3])]

    kv = project_kv(normed, normed_sib, (kv_shard, kv_x, kv_y, kv_dx, kv_dy))
    ectx, egrad = expert_attend(meta, proj, dctx, kv, factor)
    low, high = after(q_y, ectx, *wo_a)[:half], after(q_x, ectx, *wo_a)[half:]
    q_dx, q_dy = over_x(low), over_y(high)
    wo_a = jnp.stack(wo_a)
    wo_b = []
    for s in range(4):
        piece = lax.dynamic_index_in_dim(
            wo_a, chip ^ lax.rem(plane + s, 4), 0, keepdims=False
        )
        perm = [(i, (i + s) % 4) for i in range(4)]
        wo_b.append(lax.ppermute(piece, "tensor", perm) if s else piece)

    ax, ak, by, bk = weight_grads(chip_meta, pair, pair_sib, after(ectx, low, high), egrad)
    a_got, b_got = over_x(ax), over_y(by)
    ctx = attend(
        meta, normed, normed_sib, (q_shard, q_x, q_y, q_dx, q_dy), after(kv, ax), positions, factor
    )
    ctx_own, ctx_other = ctx
    wo_b = [after(x, ctx_own) for x in wo_b]
    a_got, b_got = after(a_got, ctx_own), after(b_got, ctx_own)
    ctx_got = swap(after(ctx_other, a_got, b_got, *wo_b))
    ctx_rows = jnp.concatenate([ctx_own, ctx_got], axis=1)
    turn = lambda x: lax.ppermute(x, "tensor", [(i, (i + 1) % 4) for i in range(4)])
    ctx_1 = turn(ctx_rows)
    a_sum, b_sum = ak + a_got, bk + b_got
    a_rest, b_rest = over_y(a_sum[1]), over_x(b_sum[1])
    mine = jnp.stack([a_sum[0] + a_rest, b_sum[0] + b_rest])
    wo = after(jnp.stack([after(x, ctx_got) for x in wo_b]), a_rest, b_rest)
    wo_x, wo_y = over_x(wo), over_y(wo)
    sent = after(mine, wo_x, wo_y)
    from_x, from_y = over_x(sent), over_y(sent)
    ctx_2 = turn(ctx_1)
    wo_sib = [swap(after(wo, wo_x)), swap(wo_x), swap(wo_y)]
    wo_dx = over_x(after(wo_y, from_x, from_y, wo_sib[0])[:2])
    wo_dy = over_y(after(wo_x, from_x, from_y, wo_sib[0])[2:])
    ctx_3 = turn(ctx_2)
    near = output_near(chip_meta, flat, (ctx_rows, ctx_1, ctx_2), (wo, wo_x, wo_y), wo_sib)
    far_x = over_x(after(from_y, wo_dx, wo_dy)[0])
    far_y = over_y(after(from_x, wo_dx, wo_dy)[1])
    near_grads = (mine, from_x, from_y)
    near_sib = tuple(swap(x) for x in near_grads)
    shapes = (ex_wq.shape, ex_wk.shape, ex_wv.shape, ex_wo.shape)
    grads = place_grads(chip_meta, near_grads, near_sib, shapes, range(3))
    wo_own = (wo, wo_x, wo_y, wo_dx, wo_dy)
    wo_sib += [swap(wo_dx), swap(wo_dy)]
    far = (far_x, far_y)
    grads = place_grads(chip_meta, far, [swap(x) for x in far], shapes, range(3, 4), grads)
    out = output_far(chip_meta, near, (ctx_rows, ctx_1, ctx_2, ctx_3), wo_own, wo_sib)
    return (out.reshape(samples, positions, -1), *grads)


def fits_plane(mesh):
    return mesh.shape["dp"] == 8 and mesh.shape["tensor"] == 4


def solution(mesh):
    in_specs = (
        P("dp", None, None),
        P("dp"),
        P("dp"),
        P("dp"),
        P("dp", "tensor"),
        P("dp", "tensor"),
        P("dp", "tensor"),
        P("tensor", "dp"),
        P("dp", None, None),
        P(None, "tensor"),
        P(None, "tensor"),
        P(None, "tensor"),
        P("tensor", None),
        P("dp", None, None),
    )
    out_specs = (
        P("dp", None, "tensor"),
        P(None, "tensor"),
        P(None, "tensor"),
        P(None, "tensor"),
        P("tensor", None),
    )
    body = plane_body if fits_plane(mesh) else general_body
    return jax.shard_map(body, mesh=mesh, in_specs=in_specs, out_specs=out_specs, check_vma=False)
```
